128 devices in a mesh: gx: 4 (over y), gy: 32 (over z, x, core).
Axes of the slice: x: 4, y: 4, z: 4, core: 2. Of those that a mesh axis runs over, the one named last changes fastest.
Arguments:
- multipoles: bfloat16 [16384, 216], P(('gx', 'gy')), may hold values from -6 to 6
- operators: bfloat16 [216, 27648], replicated, may hold values from -0.009765625 to 0.009765625
- coarse_local: float32 [512, 216], P(('gx', 'gy')), may hold values from -1.5 to 1.5
- positions: float32 [16384, 3, 128], P(('gx', 'gy')), may hold values from -1 to 1
- charges: float32 [16384, 128], P(('gx', 'gy')), may hold values from -0.18 to 0.18
- coarse_coords: float32 [16384, 3, 128], P(('gx', 'gy')), may hold values from -1 to 1
- box_count: int32 [128], replicated, may hold values from 64 to 128, as said below
- particle_count: int32 [16384], P(('gx', 'gy')), may hold values from 0 to 128, as said below
- expansion_sends: int32 [128, 128, 32], P(('gx', 'gy')), may hold values from -1 to 127, as said below
- far_list: int32 [16384, 128], P(('gx', 'gy')), may hold values from -1 to 4223, as said below
- block_sends: int32 [128, 128, 8], P(('gx', 'gy')), may hold values from -1 to 127, as said below
- near_list: int32 [16384, 13], P(('gx', 'gy')), may hold values from -1 to 1151, as said below
- near_offset: int32 [16384, 13], P(('gx', 'gy')), may hold values from 0 to 25
Outputs:
- potential: float32 [16384, 128], P(('gx', 'gy'))
- local_expansion: float32 [216, 16384], P(None, ('gx', 'gy'))
The draws below stay inside these ranges and needn't reach their ends.
Inputs may be any that keep to these rules, and one draw needn't show every extreme that they name: Device d owns the boxes box_start[d] to box_start[d] + box_count[d] - 1 of the window's Morton order, in its first box_count[d] slots; the counts sum to 12288, and some device owns 128 boxes. `particle_count`: slots that hold a box have 1 to 128 particles, and every device has a box with 128; the other slots have 0. `expansion_sends`: entry [p, d, :] names slots of boxes of device p, filled from the start and -1 after; it is all -1 unless p != d and either |p - d| <= 4 or p and d differ in one bit; every device sends 32 to some device and receives 32 from some device. `far_list`: an entry of a slot that holds a box names a row of its device's expansion table that holds a box; every entry of a slot without a box is -1. `block_sends`: entry [p, d, :] names slots of boxes of device p, filled from the start and -1 after; it is all -1 unless p != d and either |p - d| <= 4 or p and d differ in one bit; every device sends 8 to some device and receives 8 from some device. `near_list`: an entry of a slot that holds a box names a row of its device's block table that holds a box; every entry of a slot without a box is -1.
All inputs are finite; a program needn't handle non-finite values.
Results may differ from the reference program's by a relative error of at most 0.0014.
Values may be sent and summed in bfloat16 or wider, within the bound.
No kernel may reach another device: no remote copies, remote signals or barrier semaphores. Data moves between devices by JAX's collectives and lax.ppermute only.
A program may use at most 128 MiB of HBM per device.

```python
import jax
import jax.numpy as jnp
from jax import lax

ORDER = 6
NCOEF = 216
PB = 128
NOFF = 128
NNB = 13
BOX_CAP = 128
BOX_MEAN = 96
MCAP = 32
NCAP = 8
NDEV = 128
SLOTS = 16384
NCOARSE = 512


def box_layout(key):
    key = jax.random.fold_in(key, 101)
    spread = jax.random.randint(key, (NDEV // 2,), 0, BOX_CAP // 4 + 1)
    spread = spread.at[0].set(BOX_CAP // 4)
    counts = jnp.concatenate([BOX_MEAN + spread, BOX_MEAN - spread])
    shuffle = jax.random.permutation(jax.random.fold_in(key, 1), NDEV)
    return counts[shuffle].astype(jnp.int32)


def peer_candidates():
    devices = jnp.arange(NDEV, dtype=jnp.int32)
    columns = []
    for delta in (-4, -3, -2, -1, 1, 2, 3, 4):
        shifted = devices + delta
        inside = (shifted >= 0) & (shifted < NDEV)
        columns.append(jnp.where(inside, shifted, devices ^ 1))
    for bit_number in range(NDEV.bit_length() - 1):
        columns.append(devices ^ 1 << bit_number)
    return jnp.stack(columns, axis=1).astype(jnp.int32)


def send_plan(key, label_code, capacity):
    counts = box_layout(key)
    candidates = peer_candidates()
    devices = jnp.arange(NDEV, dtype=jnp.int32)
    active_recv = jnp.any(candidates[:, :, None] == devices[None, None, :], axis=1)
    active = active_recv.T
    key = jax.random.fold_in(key, label_code)
    filled = jax.random.randint(key, (NDEV, NDEV), max(1, capacity // 2), capacity + 1)
    full_pair = devices[None, :] == (devices ^ 1)[:, None]
    filled = jnp.where(full_pair, capacity, filled)
    filled = jnp.where(active, filled, 0)
    chosen = jax.random.randint(jax.random.fold_in(key, 2), (NDEV, NDEV, capacity), 0, counts[:, None, None])
    column = jnp.arange(capacity)[None, None, :]
    send_table = jnp.where(column < filled[:, :, None], chosen, -1)
    return (counts, filled, candidates, send_table.astype(jnp.int32))


def list_plan(key, label_code, capacity, list_width, own_num, own_den):
    counts, filled, candidates, send_table = send_plan(key, label_code, capacity)
    key = jax.random.fold_in(key, label_code + 50)
    shape_all = (NDEV, BOX_CAP, list_width)
    receiver = jnp.arange(NDEV)[:, None, None]
    pick = jax.random.randint(key, shape_all, 0, candidates.shape[1])
    remote_peer = candidates[receiver, pick]
    own_flag = jax.random.randint(jax.random.fold_in(key, 3), shape_all, 0, own_den) < own_num
    own_entry = jax.random.randint(jax.random.fold_in(key, 1), shape_all, 0, counts[:, None, None])
    reach_count = filled[remote_peer, receiver]
    remote = BOX_CAP + remote_peer * capacity + jax.random.randint(jax.random.fold_in(key, 2), shape_all, 0, reach_count)
    table_entry = jnp.where(own_flag, own_entry, remote)
    live_box = jnp.arange(BOX_CAP)[None, :, None] < counts[:, None, None]
    return jnp.where(live_box, table_entry, -1).reshape(NDEV * BOX_CAP, list_width).astype(jnp.int32)


def draw_box_count(key, part):
    return box_layout(key)


def draw_particle_count(key, part):
    counts = box_layout(key)
    key = jax.random.fold_in(key, 401)
    sizes_drawn = jax.random.randint(key, (NDEV, BOX_CAP), 1, PB + 1)
    full_slot = jax.random.randint(jax.random.fold_in(key, 1), (NDEV,), 0, counts)
    slot_ids = jnp.arange(BOX_CAP)[None, :]
    sizes_drawn = jnp.where(slot_ids == full_slot[:, None], PB, sizes_drawn)
    return jnp.where(slot_ids < counts[:, None], sizes_drawn, 0).reshape(NDEV * BOX_CAP).astype(jnp.int32)


def draw_expansion_sends(key, part):
    return send_plan(key, 211, MCAP)[3]


def draw_far_list(key, part):
    return list_plan(key, 211, MCAP, NOFF, 2, 5)


def draw_block_sends(key, part):
    return send_plan(key, 307, NCAP)[3]


def draw_near_list(key, part):
    return list_plan(key, 307, NCAP, NNB, 1, 2)


def touch_ends(values, key, low, high):
    longest = values.shape.index(max(values.shape))
    spots = []
    for shift in (0, 1):
        where = [jax.random.randint(jax.random.fold_in(key, axis), (), 0, length) for axis, length in enumerate(values.shape)]
        where[longest] = (where[longest] + shift) % values.shape[longest]
        spots.append(tuple(where))
    return values.at[spots[0]].set(low).at[spots[1]].set(high)


def level_of(own_key, extent, split, low, largest):
    factor_of, own = 1.0, jax.random.fold_in(own_key, 6)
    for axis_at, blocks in split:
        steps = jnp.exp(jax.random.uniform(jax.random.fold_in(own, axis_at), (blocks,), jnp.float32, low / len(split), largest / len(split)))
        factor_of = factor_of * jnp.repeat(steps, extent[axis_at] // blocks).reshape([-1 if axis == axis_at else 1 for axis in range(len(extent))])
    return factor_of


def scatter_about(stream_key, dims, deviation, reach, pieces=(), kind=jnp.bfloat16):
    values = deviation * jax.random.normal(stream_key, dims, jnp.float32)
    if pieces:
        values = values * level_of(stream_key, dims, pieces, -0.22, 0.18)
    return jnp.clip(values, -reach, reach).astype(kind)


def setup_inputs(seed: int = 0) -> dict:
    key_list = jax.random.split(jax.random.key(seed), 14)
    multipoles = scatter_about(key_list[0], (SLOTS, NCOEF), 1.0, 6.0, ((0, 128),))
    operators = scatter_about(key_list[1], (NCOEF, NOFF * NCOEF), (NOFF * NCOEF * 16) ** -0.5, 0.009765625)
    coarse_local = scatter_about(key_list[2], (NCOARSE, NCOEF), 0.25, 1.5, ((0, 128),), jnp.float32)
    positions = jnp.clip(jax.random.uniform(key_list[3], (SLOTS, 3, PB), jnp.float32, -1.0, 1.0) * level_of(key_list[3], (SLOTS, 3, PB), ((0, 128),), -0.4, 0.0), -1.0, 1.0)
    charges = scatter_about(key_list[4], (SLOTS, PB), 0.03, 0.18, ((0, 128),), jnp.float32)
    coarse_coords = jnp.clip(jax.random.uniform(key_list[5], (SLOTS, 3, PB), jnp.float32, -1.0, 1.0) * level_of(key_list[5], (SLOTS, 3, PB), ((0, 128),), -0.4, 0.0), -1.0, 1.0)
    box_count = draw_box_count(jax.random.fold_in(key_list[13], 71), 0)
    particle_count = draw_particle_count(jax.random.fold_in(key_list[13], 71), 0)
    expansion_sends = draw_expansion_sends(jax.random.fold_in(key_list[13], 71), 0)
    far_list = draw_far_list(jax.random.fold_in(key_list[13], 71), 0)
    block_sends = draw_block_sends(jax.random.fold_in(key_list[13], 71), 0)
    near_list = draw_near_list(jax.random.fold_in(key_list[13], 71), 0)
    near_offset = touch_ends(jax.random.randint(key_list[12], (SLOTS, NNB), 0, 26), jax.random.fold_in(key_list[12], 1), 0, 25).astype(jnp.int32)
    return {"multipoles": multipoles, "operators": operators, "coarse_local": coarse_local, "positions": positions, "charges": charges, "coarse_coords": coarse_coords, "box_count": box_count, "particle_count": particle_count, "expansion_sends": expansion_sends, "far_list": far_list, "block_sends": block_sends, "near_list": near_list, "near_offset": near_offset}


SOFTENING = 0.01

def chebyshev(values, degree_count):
    series = [jnp.ones_like(values), values]
    for degree in range(2, degree_count):
        series.append(2.0 * values * series[-1] - series[-2])
    return jnp.stack(series[:degree_count], axis=-2)

def evaluate(coeffs, coordinates):
    box_total = coeffs.shape[0]
    coeff_grid = coeffs.reshape(box_total, ORDER, ORDER, ORDER)
    along_x = chebyshev(coordinates[:, 0], ORDER)
    along_y = chebyshev(coordinates[:, 1], ORDER)
    along_z = chebyshev(coordinates[:, 2], ORDER)
    folded = jnp.einsum('bxyz,bzi->bxyi', coeff_grid, along_z, precision=lax.Precision.HIGHEST)
    folded = lax.optimization_barrier(jnp.sum(folded * along_y[:, None], axis=2))
    return lax.optimization_barrier(jnp.sum(folded * along_x, axis=1))

def pair_kernel(targets, sources, offset_vec):
    shifted = sources + offset_vec[:, :, None]
    separation = targets[:, :, :, None] - shifted[:, :, None, :]
    dist_sq = lax.optimization_barrier(jnp.sum(separation * separation, axis=1)) + SOFTENING
    return lax.rsqrt(dist_sq)

def displacement(offset_code):
    full_code = offset_code + (offset_code >= 13).astype(jnp.int32)
    step_x = full_code // 9 - 1
    step_y = full_code // 3 % 3 - 1
    step_z = full_code % 3 - 1
    return 2.0 * jnp.stack([step_x, step_y, step_z], axis=1).astype(jnp.float32)

def reference(multipoles, operators, coarse_local, positions, charges, coarse_coords, box_count, particle_count, expansion_sends, far_list, block_sends, near_list, near_offset):
    slot_ids = lax.broadcasted_iota(jnp.int32, charges.shape, 1)
    live_mask = slot_ids < particle_count[:, None]
    masked_charge = jnp.where(live_mask, charges, 0.0)
    blocks = jnp.concatenate([positions, masked_charge[:, None, :]], axis=1)
    device_ids = jnp.arange(NDEV, dtype=jnp.int32)
    box_ids = jnp.arange(BOX_CAP, dtype=jnp.int32)
    off_diag = 1.0 - jnp.eye(PB, dtype=jnp.float32)

    def table_ids(send_table, device, capacity):
        column = send_table[:, device, :]
        remote = device_ids[:, None] * BOX_CAP + column
        remote = jnp.where(column < 0, -1, remote)
        return jnp.concatenate([device * BOX_CAP + box_ids, remote.reshape(NDEV * capacity)]).astype(jnp.int32)

    def lookup(row_table, entries):
        chosen = row_table[jnp.maximum(entries, 0)]
        return jnp.where(entries < 0, -1, chosen)

    def one_device(device):
        first_slot = (device * BOX_CAP).astype(jnp.int32)
        far_entries = lax.dynamic_slice_in_dim(far_list, first_slot, BOX_CAP, 0)
        far_rows = lookup(table_ids(expansion_sends, device, MCAP), far_entries)
        gathered = jnp.where((far_rows >= 0)[:, :, None], multipoles[jnp.maximum(far_rows, 0)], jnp.zeros((), multipoles.dtype))
        local_exp = lax.dot_general(operators, gathered.reshape(BOX_CAP, NOFF * NCOEF), (((1,), (1,)), ((), ())), preferred_element_type=jnp.float32)
        own_pos = lax.dynamic_slice_in_dim(positions, first_slot, BOX_CAP, 0)
        own_charge = lax.dynamic_slice_in_dim(masked_charge, first_slot, BOX_CAP, 0)
        own_live = lax.dynamic_slice_in_dim(live_mask, first_slot, BOX_CAP, 0)
        own_coarse = lax.dynamic_slice_in_dim(coarse_coords, first_slot, BOX_CAP, 0)
        near_entries = lax.dynamic_slice_in_dim(near_list, first_slot, BOX_CAP, 0)
        near_codes = lax.dynamic_slice_in_dim(near_offset, first_slot, BOX_CAP, 0)
        near_rows = lookup(table_ids(block_sends, device, NCAP), near_entries)
        self_kernel = pair_kernel(own_pos, own_pos, jnp.zeros((BOX_CAP, 3), jnp.float32))
        near_pot = lax.optimization_barrier(jnp.sum(self_kernel * off_diag * own_charge[:, None, :], axis=2))

        def neighbour(running, columns):
            rows_now, codes_now = columns
            source = jnp.where((rows_now >= 0)[:, None, None], blocks[jnp.maximum(rows_now, 0)], 0.0)
            kernel = pair_kernel(own_pos, source[:, :3], displacement(codes_now))
            return (running + lax.optimization_barrier(jnp.sum(kernel * source[:, 3][:, None, :], axis=2)), None)
        near_pot, unused = lax.scan(neighbour, near_pot, (near_rows.T, near_codes.T))
        far_pot = evaluate(local_exp.T, own_pos)
        box_start = jnp.sum(jnp.where(device_ids < device, box_count, 0))
        ancestor = ((box_start + box_ids) % NCOARSE).astype(jnp.int32)
        coarse_pot = evaluate(coarse_local[ancestor], own_coarse)
        potential = jnp.where(own_live, near_pot + far_pot + coarse_pot, 0.0)
        return (potential, local_exp)
    potential, local_exp = lax.map(one_device, device_ids)
    return (potential.reshape(SLOTS, PB), jnp.transpose(local_exp, (1, 0, 2)).reshape(NCOEF, SLOTS))
```

```python
import functools

import jax
import jax.numpy as jnp
from jax import lax
from jax.experimental import pallas as pl
from jax.experimental.pallas import tpu as pltpu
from jax.sharding import PartitionSpec as P

ORDER = 6
SOFTENING = 0.01
COEFFS = 216
SLOTS = 128
LINE = 32
UNIT = 96
LEVEL3 = 16
TABLE = 512
NEAR_ROWS = 232
EMPTY = 224
STEPS = (-4, -3, -2, -1, 1, 2, 3, 4)
PER_STEP = 16
VMEM = pltpu.CompilerParams(vmem_limit_bytes=56 * 1024 * 1024)


def iota(shape, dim):
    return lax.broadcasted_iota(jnp.int32, shape, dim)


def position():
    line, place = lax.axis_index("gx"), lax.axis_index("gy")
    return line, place, line * LINE + place


def peer_slot(owner, device):
    delta = owner - device
    cross = owner ^ device
    far = jnp.where(cross == 8, 8, jnp.where(cross == 16, 9, jnp.where(cross == 32, 10, 11)))
    near = jnp.where(delta < 0, delta + 4, delta + 3)
    return jnp.where((delta >= -4) & (delta <= 4), near, far)


def contract(a, b, dims):
    return lax.dot_general(a, b, ((dims[:1], dims[1:]), ((), ())), preferred_element_type=jnp.float32)


def pack_kernel(mult, exp_sends, block_sends, pos, charges, counts, coarse, near_list, near_offset,
                gy_out, gx_out, masked_out, lists_out):
    line, place, device = position()
    lanes = iota((SLOTS, SLOTS), 1)
    count_col = jnp.transpose(jnp.broadcast_to(counts[...], (SLOTS, SLOTS)).astype(jnp.float32))
    masked = jnp.where(lanes.astype(jnp.float32) < count_col, charges[...], 0.0)
    masked_out[...] = masked

    targets = [device + step for step in STEPS] + [device ^ bit for bit in (8, 16, 32, 64)]

    def picks(table):
        rows = table.shape[0]
        values = table[...].astype(jnp.float32)
        lane = iota((rows, SLOTS), 1)
        out = []
        for target in targets:
            column = jnp.sum(jnp.where(lane == target, values, 0.0), axis=1, keepdims=True)
            out.append(jnp.where(column == lane.astype(jnp.float32), 1.0, 0.0))
        return jnp.concatenate(out, axis=0).astype(jnp.bfloat16)

    rows = contract(picks(exp_sends), mult[...], (1, 1))
    low = rows[:, :SLOTS]
    high = jnp.concatenate([rows[:, SLOTS:], jnp.zeros((rows.shape[0], 256 - COEFFS), jnp.float32)], axis=1)
    block_picks = picks(block_sends)
    planes = [pos[0], pos[1], pos[2], masked]
    fields = [contract(block_picks, plane.astype(jnp.bfloat16), (1, 0)) for plane in planes]

    def unit(j):
        parts = [low[32 * j:32 * j + 32], high[32 * j:32 * j + 32]]
        parts += [field[8 * j:8 * j + 8] for field in fields]
        return jnp.concatenate(parts, axis=0).astype(jnp.bfloat16)

    for j, step in enumerate(STEPS):
        value = unit(j)
        there = place + step
        inside = (there >= 0) & (there < LINE)

        @pl.when(inside)
        def _():
            gy_out[there, 0:UNIT, :] = value

        to_line = line + (1 if step > 0 else -1)

        @pl.when(jnp.logical_not(inside) & (to_line >= 0) & (to_line < 4))
        def _():
            part = (there - LINE) if step > 0 else (there + 4)
            gx_out[to_line, pl.ds(pl.multiple_of(UNIT + UNIT * part, UNIT), UNIT), :] = value

    gy_out[place ^ 8, 0:UNIT, :] = unit(8)
    gy_out[place ^ 16, 0:UNIT, :] = unit(9)
    gx_out[line ^ 1, 0:UNIT, :] = unit(10)
    gx_out[line ^ 2, 0:UNIT, :] = unit(11)

    table = coarse[...]
    hi = table.astype(jnp.bfloat16).astype(jnp.float32)
    pieces = []
    for part in (hi, table - hi):
        pieces += [part[:, :SLOTS], jnp.concatenate([part[:, SLOTS:], jnp.zeros((4, 256 - COEFFS), jnp.float32)], axis=1)]
    piece = jnp.concatenate(pieces, axis=0).astype(jnp.bfloat16)
    for other in range(4):
        gx_out[other, 5 * UNIT:5 * UNIT + LEVEL3, :] = piece

    entries = near_list[...]
    remote = entries - SLOTS
    compact = SLOTS + 8 * peer_slot(remote >> 3, device) + (remote & 7)
    row = jnp.where(entries < 0, EMPTY, jnp.where(entries < SLOTS, entries, compact))
    codes = near_offset[...]
    codes = codes + jnp.where(codes >= 13, 1, 0)
    lists_out[0:13, :] = row * 32 + codes


def pack(mult, exp_sends, block_sends, pos, charges, counts, coarse, near_list, near_offset):
    return pl.pallas_call(
        pack_kernel,
        out_shape=(
            jax.ShapeDtypeStruct((LINE, UNIT + LEVEL3, SLOTS), jnp.bfloat16),
            jax.ShapeDtypeStruct((4, 5 * UNIT + LEVEL3, SLOTS), jnp.bfloat16),
            jax.ShapeDtypeStruct((SLOTS, SLOTS), jnp.float32),
            jax.ShapeDtypeStruct((16, SLOTS), jnp.int32),
        ),
        compiler_params=VMEM,
        name="pack",
    )(mult, exp_sends, block_sends, pos, charges, counts, coarse, near_list, near_offset)


def forward_kernel(gy_in, received, box_count, gy_out, picked, sems):
    line, place, device = position()
    edge = (place >= LINE - 4) | (place < 4)
    upper = place >= LINE - 4
    source = jnp.where(upper, jnp.maximum(line - 1, 0), jnp.minimum(line + 1, 3))
    base = jnp.where(upper, 0, LINE - 4)

    def forwards(part):
        return pltpu.make_async_copy(
            received.at[source, UNIT + UNIT * part:2 * UNIT + UNIT * part, :],
            gy_out.at[base + part, 0:UNIT, :],
            sems.at[part],
        )

    @pl.when(edge)
    def _():
        for part in range(4):
            forwards(part).start()

    pieces = [received[other, 5 * UNIT:5 * UNIT + LEVEL3, :] for other in range(4)]
    table = jnp.concatenate(pieces, axis=0)
    total = LINE * LEVEL3
    row = iota((total, SLOTS), 0)
    before = iota((total, SLOTS), 1) < line * LINE + (row >> 4)
    counts = jnp.broadcast_to(box_count[...].astype(jnp.float32), (total, SLOTS))
    start = jnp.sum(jnp.where(before, counts, 0.0), axis=1, keepdims=True).astype(jnp.int32)
    start = jnp.broadcast_to(start, (total, 4 * LEVEL3))
    row = iota((total, 4 * LEVEL3), 0)
    member = start + ((4 * place + (row & 3) - start) & 127)
    wanted = ((member & 511) >> 7) * LEVEL3 + (row & 15)
    choose = jnp.where(iota((total, 4 * LEVEL3), 1) == wanted, 1.0, 0.0).astype(jnp.bfloat16)
    picked[...] = contract(choose, table, (1, 0)).astype(jnp.bfloat16).reshape(LINE, LEVEL3, SLOTS)
    level3 = pltpu.make_async_copy(picked, gy_out.at[:, UNIT:UNIT + LEVEL3, :], sems.at[4])
    level3.start()
    level3.wait()

    @pl.when(edge)
    def _():
        for part in range(4):
            forwards(part).wait()


def forward(gy_buffer, received, box_count):
    whole = pl.BlockSpec(memory_space=pltpu.VMEM)
    return pl.pallas_call(
        forward_kernel,
        out_shape=jax.ShapeDtypeStruct(gy_buffer.shape, gy_buffer.dtype),
        in_specs=[pl.BlockSpec(memory_space=pl.ANY), whole, whole],
        out_specs=pl.BlockSpec(memory_space=pl.ANY),
        scratch_shapes=[pltpu.VMEM((LINE, LEVEL3, SLOTS), jnp.bfloat16), pltpu.SemaphoreType.DMA((5,))],
        input_output_aliases={0: 0},
        compiler_params=VMEM,
        name="forward",
    )(gy_buffer, received, box_count)


def peers(gy_recv, gx_recv, line, place, device):
    out = []
    for step in STEPS:
        there = device + step
        out.append((gy_recv.at[(place + step) & (LINE - 1)], (there >= 0) & (there < 4 * LINE)))
    for bit in (8, 16):
        out.append((gy_recv.at[place ^ bit], None))
    for bit in (1, 2):
        out.append((gx_recv.at[line ^ bit], None))
    return out


def series(u):
    terms = [None, u]
    terms.append(2.0 * u * u - 1.0)
    for degree in range(3, ORDER):
        terms.append(2.0 * u * terms[-1] - terms[-2])
    return terms


def evaluate(coeffs, coords, rows):
    along_x, along_y, along_z = [series(c) for c in coords]

    def line_of(k):
        return jnp.broadcast_to(coeffs[k:k + 1, :], (rows, SLOTS))

    total = None
    for a in range(ORDER):
        plane = None
        for b in range(ORDER):
            base = (a * ORDER + b) * ORDER
            value = line_of(base)
            for c in range(1, ORDER):
                value = value + line_of(base + c) * along_z[c]
            if b:
                value = value * along_y[b]
            plane = value if plane is None else plane + value
        if a:
            plane = plane * along_x[a]
        total = plane if total is None else total + plane
    return total


def far_kernel(mult, gy_recv, gx_recv, far_list, box_count, pos, coarse_coords, operators,
               local_out, eval_out, table, entries, picked, pos_t, coarse_t, level3):
    line, place, device = position()
    step = pl.program_id(0)

    @pl.when(step == 0)
    def _():
        low, high = [], []
        for message, valid in peers(gy_recv, gx_recv, line, place, device):
            lo = message[0:32, :].astype(jnp.float32)
            hi = message[32:64, :].astype(jnp.float32)
            if valid is not None:
                lo = jnp.where(valid, lo, 0.0)
                hi = jnp.where(valid, hi, 0.0)
            low.append(lo)
            high.append(hi)
        low = jnp.transpose(jnp.concatenate(low, axis=0))
        high = jnp.transpose(jnp.concatenate(high, axis=0))
        table[:, SLOTS:] = jnp.concatenate([low, high[:COEFFS - SLOTS]], axis=0).astype(jnp.bfloat16)
        table[:, :SLOTS] = mult[...]
        listed = far_list[...]
        remote = listed - SLOTS
        compact = SLOTS + 32 * peer_slot(remote >> 5, device) + (remote & 31)
        compact = jnp.where(listed < SLOTS, listed, compact)
        entries[...] = jnp.transpose(compact.astype(jnp.float32)).astype(jnp.int32)
        local_out[...] = jnp.zeros_like(local_out)

    lines = iota((TABLE, SLOTS), 0)
    for pair in range(PER_STEP // 2):
        first = step * PER_STEP + 2 * pair
        hot = []
        for which in range(2):
            wanted = entries[pl.ds(first + which, 1), :]
            hot.append(jnp.where(lines == wanted, 1.0, 0.0).astype(jnp.bfloat16))
        found = contract(table[...], jnp.concatenate(hot, axis=1), (1, 0))
        found = jnp.concatenate([found[:, :SLOTS], found[:, SLOTS:]], axis=0)
        picked[2 * COEFFS * pair:2 * COEFFS * (pair + 1), :] = found.astype(jnp.bfloat16)
    local_out[...] += contract(operators[...], picked[...], (1, 0))

    @pl.when(step == pl.num_programs(0) - 1)
    def _():
        for axis in range(3):
            pos_t[axis] = jnp.transpose(pos[axis])
            coarse_t[axis] = jnp.transpose(coarse_coords[axis])
        before = iota((1, SLOTS), 1) < device
        start = jnp.sum(jnp.where(before, box_count[...].astype(jnp.float32), 0.0), axis=1, keepdims=True)
        start = jnp.broadcast_to(start.astype(jnp.int32), (TABLE, SLOTS))
        pieces = gy_recv[:, UNIT:UNIT + LEVEL3, :].reshape(TABLE, SLOTS)
        pieces = jnp.transpose(pieces.astype(jnp.float32)).astype(jnp.bfloat16)
        row = iota((TABLE, SLOTS), 0)
        member = (row >> 4) * 4 + (row & 3)
        hit = member == ((start + iota((TABLE, SLOTS), 1)) & 127)
        for half in range(2):
            order = jnp.where(hit & (((row >> 2) & 1) == half), 1.0, 0.0).astype(jnp.bfloat16)
            part = contract(pieces, order, (1, 0))
            if half:
                level3[SLOTS:, :] = part[:COEFFS - SLOTS]
            else:
                level3[:SLOTS, :] = part

        rows = 16

        @pl.loop(0, SLOTS // rows)
        def _(index):
            here = pl.ds(pl.multiple_of(index * rows, rows), rows)
            far = evaluate(local_out, [pos_t[axis, here, :] for axis in range(3)], rows)
            coarse = evaluate(level3, [coarse_t[axis, here, :] for axis in range(3)], rows)
            eval_out[here, :] = far + coarse


def far_field(mult, gy_recv, gx_recv, far_list, box_count, pos, coarse_coords, operators):
    steps = SLOTS // PER_STEP
    whole = pl.BlockSpec(memory_space=pltpu.VMEM)

    def const(shape):
        return pl.BlockSpec(shape, lambda i: (0,) * len(shape))

    return pl.pallas_call(
        far_kernel,
        grid=(steps,),
        out_shape=(
            jax.ShapeDtypeStruct((COEFFS, SLOTS), jnp.float32),
            jax.ShapeDtypeStruct((SLOTS, SLOTS), jnp.float32),
        ),
        in_specs=[whole] * 7 + [pl.BlockSpec((COEFFS, PER_STEP * COEFFS), lambda i: (0, i))],
        out_specs=(const((COEFFS, SLOTS)), const((SLOTS, SLOTS))),
        scratch_shapes=[
            pltpu.VMEM((COEFFS, TABLE), jnp.bfloat16),
            pltpu.VMEM((SLOTS, SLOTS), jnp.int32),
            pltpu.VMEM((PER_STEP * COEFFS, SLOTS), jnp.bfloat16),
            pltpu.VMEM((3, SLOTS, SLOTS), jnp.float32),
            pltpu.VMEM((3, SLOTS, SLOTS), jnp.float32),
            pltpu.VMEM((COEFFS, SLOTS), jnp.float32),
        ],
        compiler_params=pltpu.CompilerParams(
            vmem_limit_bytes=56 * 1024 * 1024, dimension_semantics=("arbitrary",)
        ),
        name="far",
    )(mult, gy_recv, gx_recv, far_list, box_count, pos, coarse_coords, operators)


def near_kernel(lists, counts, pos, masked, gy_recv, gx_recv, eval_in, count_row, out,
                blocks, shifts, sources, norms, pos_t, total):
    line, place, device = position()
    lane8 = iota((8, SLOTS), 1)
    row8 = iota((8, SLOTS), 0)

    for axis in range(3):
        pos_t[axis] = jnp.transpose(pos[axis])
        blocks[0:SLOTS, axis, :] = pos[axis]
    blocks[0:SLOTS, 3, :] = masked[...]
    for j, (message, valid) in enumerate(peers(gy_recv, gx_recv, line, place, device)):
        value = message[64:UNIT, :].astype(jnp.float32)
        for field in range(4):
            blocks[SLOTS + 8 * j:SLOTS + 8 * j + 8, field, :] = value[8 * field:8 * field + 8]
    blocks[EMPTY] = jnp.zeros((8, SLOTS), jnp.float32)
    for code in range(27):
        moves = [2.0 * (code // 9 - 1), 2.0 * (code // 3 % 3 - 1), 2.0 * (code % 3 - 1)]
        value = jnp.zeros((8, SLOTS), jnp.float32)
        for axis in range(3):
            if moves[axis]:
                value = jnp.where(row8 == axis, moves[axis], value)
        shifts[code] = value
    total[...] = eval_in[...]

    @pl.loop(0, SLOTS)
    def _(box):
        live = counts[box]

        @pl.when(live > 0)
        def _():
            for n in range(14):
                if n < 13:
                    code = lists[n, box]
                    value = blocks[code >> 5] + shifts[code & 31]
                else:
                    value = blocks[box]
                square = value * value
                sources[n] = value
                norms[n] = square + pltpu.roll(square, 1, 0) + pltpu.roll(square, 2, 0)

            pick = jnp.full((8, SLOTS), box, jnp.int32)

            @pl.loop(0, (live + 31) >> 5)
            def _(chunk):
                base = pl.multiple_of(chunk * 32, 32)
                points, bases, sums = [], [], []
                for v in range(4):
                    mine = [
                        jnp.take_along_axis(pos_t[axis, pl.ds(base + 8 * v, 8), :], pick, axis=1, mode="promise_in_bounds")
                        for axis in range(3)
                    ]
                    bases.append(mine[0] * mine[0] + mine[1] * mine[1] + mine[2] * mine[2] + SOFTENING)
                    points.append([-2.0 * m for m in mine])
                    sums.append(jnp.zeros((8, SLOTS), jnp.float32))
                for n in range(14):
                    fields = [jnp.broadcast_to(sources[n, f:f + 1, :], (8, SLOTS)) for f in range(4)]
                    norm = jnp.broadcast_to(norms[n, 2:3, :], (8, SLOTS))
                    for v in range(4):
                        dist = bases[v] + norm
                        for axis in range(3):
                            dist = dist + points[v][axis] * fields[axis]
                        kernel = lax.rsqrt(dist)
                        if n == 13:
                            kernel = jnp.where(lane8 - row8 == base + 8 * v, 0.0, kernel)
                        sums[v] = sums[v] + kernel * fields[3]
                for v in range(4):
                    here = pl.ds(base + 8 * v, 8)
                    value = jnp.sum(sums[v], axis=1, keepdims=True)
                    old = total[here, :]
                    total[here, :] = jnp.where(lane8 == box, old + value, old)

    live_mask = iota((SLOTS, SLOTS), 0) < jnp.broadcast_to(count_row[...], (SLOTS, SLOTS))
    out[...] = jnp.transpose(jnp.where(live_mask, total[...], 0.0))


def near_field(lists, counts, pos, masked, gy_recv, gx_recv, eval_in, count_row):
    whole = pl.BlockSpec(memory_space=pltpu.VMEM)
    scalars = pl.BlockSpec(memory_space=pltpu.SMEM)
    return pl.pallas_call(
        near_kernel,
        out_shape=jax.ShapeDtypeStruct((SLOTS, SLOTS), jnp.float32),
        in_specs=[scalars, scalars] + [whole] * 6,
        out_specs=whole,
        scratch_shapes=[
            pltpu.VMEM((NEAR_ROWS, 8, SLOTS), jnp.float32),
            pltpu.VMEM((32, 8, SLOTS), jnp.float32),
            pltpu.VMEM((14, 8, SLOTS), jnp.float32),
            pltpu.VMEM((14, 8, SLOTS), jnp.float32),
            pltpu.VMEM((3, SLOTS, SLOTS), jnp.float32),
            pltpu.VMEM((SLOTS, SLOTS), jnp.float32),
        ],
        compiler_params=VMEM,
        name="near",
    )(lists, counts, pos, masked, gy_recv, gx_recv, eval_in, count_row)


def on_device(
    multipoles,
    operators,
    coarse_local,
    positions,
    charges,
    coarse_coords,
    box_count,
    particle_count,
    expansion_sends,
    far_list,
    block_sends,
    near_list,
    near_offset,
):
    mult = multipoles.T
    pos = jnp.transpose(positions, (1, 0, 2))
    coarse_pos = jnp.transpose(coarse_coords, (1, 0, 2))
    count_row = particle_count.reshape(1, SLOTS)
    box_row = box_count.reshape(1, SLOTS)
    gy_buffer, gx_buffer, masked, lists = pack(
        mult, expansion_sends[0].T, block_sends[0].T, pos, charges, count_row, coarse_local,
        near_list.T, near_offset.T,
    )
    gx_recv = lax.all_to_all(gx_buffer, "gx", 0, 0, tiled=True)
    gy_buffer = forward(gy_buffer, gx_recv, box_row)
    gy_recv = lax.all_to_all(gy_buffer, "gy", 0, 0, tiled=True)
    local_exp, evaluated = far_field(mult, gy_recv, gx_recv, far_list, box_row, pos, coarse_pos, operators)
    potential = near_field(lists, particle_count, pos, masked, gy_recv, gx_recv, evaluated, count_row)
    return (potential, local_exp)


def solution(mesh):
    both = ("gx", "gy")
    in_specs = (
        P(both, None),
        P(),
        P(both, None),
        P(both, None, None),
        P(both, None),
        P(both, None, None),
        P(),
        P(both),
        P(both, None, None),
        P(both, None),
        P(both, None, None),
        P(both, None),
        P(both, None),
    )
    out_specs = (P(both, None), P(None, both))
    return jax.shard_map(
        on_device, mesh=mesh, in_specs=in_specs, out_specs=out_specs, check_vma=False
    )
```

```python
import functools

import jax
import jax.numpy as jnp
from jax import lax
from jax.experimental import pallas as pl
from jax.experimental.pallas import tpu as pltpu
from jax.sharding import PartitionSpec as P

ORDER = 6
SOFTENING = 0.01
COEFFS = 216
SLOTS = 128
LINE = 32
UNIT = 96
LEVEL3 = 16
TABLE = 512
NEAR_ROWS = 232
EMPTY = 224
STEPS = (-4, -3, -2, -1, 1, 2, 3, 4)
PER_STEP = 16
CHUNK = 64
TOGETHER = 8
VMEM = pltpu.CompilerParams(vmem_limit_bytes=56 * 1024 * 1024)


def iota(shape, dim):
    return lax.broadcasted_iota(jnp.int32, shape, dim)


def position():
    line, place = lax.axis_index("gx"), lax.axis_index("gy")
    return line, place, line * LINE + place


def peer_slot(owner, device):
    delta = owner - device
    cross = owner ^ device
    far = jnp.where(cross == 8, 8, jnp.where(cross == 16, 9, jnp.where(cross == 32, 10, 11)))
    near = jnp.where(delta < 0, delta + 4, delta + 3)
    return jnp.where((delta >= -4) & (delta <= 4), near, far)


def contract(a, b, dims):
    return lax.dot_general(a, b, ((dims[:1], dims[1:]), ((), ())), preferred_element_type=jnp.float32)


def pack_kernel(mult, exp_sends, block_sends, pos, charges, counts, coarse, near_list, near_offset,
                gy_out, gx_out, masked_out, lists_out):
    line, place, device = position()
    lanes = iota((SLOTS, SLOTS), 1)
    count_col = jnp.transpose(jnp.broadcast_to(counts[...], (SLOTS, SLOTS)).astype(jnp.float32))
    masked = jnp.where(lanes.astype(jnp.float32) < count_col, charges[...], 0.0)
    masked_out[...] = masked

    targets = [device + step for step in STEPS] + [device ^ bit for bit in (8, 16, 32, 64)]

    def picks(table):
        rows = table.shape[0]
        values = table[...].astype(jnp.float32)
        lane = iota((rows, SLOTS), 1)
        out = []
        for target in targets:
            column = jnp.sum(jnp.where(lane == target, values, 0.0), axis=1, keepdims=True)
            out.append(jnp.where(column == lane.astype(jnp.float32), 1.0, 0.0))
        return jnp.concatenate(out, axis=0).astype(jnp.bfloat16)

    rows = contract(picks(exp_sends), mult[...], (1, 1))
    low = rows[:, :SLOTS]
    high = jnp.concatenate([rows[:, SLOTS:], jnp.zeros((rows.shape[0], 256 - COEFFS), jnp.float32)], axis=1)
    block_picks = picks(block_sends)
    planes = [pos[0], pos[1], pos[2], masked]
    fields = [contract(block_picks, plane.astype(jnp.bfloat16), (1, 0)) for plane in planes]

    def unit(j):
        parts = [low[32 * j:32 * j + 32], high[32 * j:32 * j + 32]]
        parts += [field[8 * j:8 * j + 8] for field in fields]
        return jnp.concatenate(parts, axis=0).astype(jnp.bfloat16)

    for j, step in enumerate(STEPS):
        value = unit(j)
        there = place + step
        inside = (there >= 0) & (there < LINE)

        @pl.when(inside)
        def _():
            gy_out[there, 0:UNIT, :] = value

        to_line = line + (1 if step > 0 else -1)

        @pl.when(jnp.logical_not(inside) & (to_line >= 0) & (to_line < 4))
        def _():
            part = (there - LINE) if step > 0 else (there + 4)
            gx_out[to_line, pl.ds(pl.multiple_of(UNIT + UNIT * part, UNIT), UNIT), :] = value

    gy_out[place ^ 8, 0:UNIT, :] = unit(8)
    gy_out[place ^ 16, 0:UNIT, :] = unit(9)
    gx_out[line ^ 1, 0:UNIT, :] = unit(10)
    gx_out[line ^ 2, 0:UNIT, :] = unit(11)

    table = coarse[...]
    hi = table.astype(jnp.bfloat16).astype(jnp.float32)
    pieces = []
    for part in (hi, table - hi):
        pieces += [part[:, :SLOTS], jnp.concatenate([part[:, SLOTS:], jnp.zeros((4, 256 - COEFFS), jnp.float32)], axis=1)]
    piece = jnp.concatenate(pieces, axis=0).astype(jnp.bfloat16)
    for other in range(4):
        gx_out[other, 5 * UNIT:5 * UNIT + LEVEL3, :] = piece

    entries = near_list[...]
    remote = entries - SLOTS
    compact = SLOTS + 8 * peer_slot(remote >> 3, device) + (remote & 7)
    row = jnp.where(entries < 0, EMPTY, jnp.where(entries < SLOTS, entries, compact))
    codes = near_offset[...]
    codes = codes + jnp.where(codes >= 13, 1, 0)
    lists_out[0:13, :] = row
    lists_out[16:29, :] = codes

    groups = jnp.floor((count_col + 31.0) * (1.0 / 32.0))
    other = jnp.transpose(groups)
    index = iota((SLOTS, SLOTS), 0)
    ahead = (groups > other) | ((groups == other) & (index < lanes))
    rank = jnp.sum(jnp.where(ahead, 1.0, 0.0), axis=0, keepdims=True)
    rank = jnp.transpose(jnp.broadcast_to(rank, (SLOTS, SLOTS)))
    order = jnp.sum(jnp.where(rank == lanes.astype(jnp.float32), index.astype(jnp.float32), 0.0), axis=0, keepdims=True)
    least = jnp.sum(jnp.where(groups >= lanes.astype(jnp.float32), 1.0, 0.0), axis=0, keepdims=True)
    lists_out[13:14, :] = order.astype(jnp.int32)
    lists_out[14:15, :] = least.astype(jnp.int32)


def pack(mult, exp_sends, block_sends, pos, charges, counts, coarse, near_list, near_offset):
    return pl.pallas_call(
        pack_kernel,
        out_shape=(
            jax.ShapeDtypeStruct((LINE, UNIT + LEVEL3, SLOTS), jnp.bfloat16),
            jax.ShapeDtypeStruct((4, 5 * UNIT + LEVEL3, SLOTS), jnp.bfloat16),
            jax.ShapeDtypeStruct((SLOTS, SLOTS), jnp.float32),
            jax.ShapeDtypeStruct((32, SLOTS), jnp.int32),
        ),
        compiler_params=VMEM,
        name="pack",
    )(mult, exp_sends, block_sends, pos, charges, counts, coarse, near_list, near_offset)


def forward_kernel(gy_in, received, box_count, gy_out, picked, sems):
    line, place, device = position()
    edge = (place >= LINE - 4) | (place < 4)
    upper = place >= LINE - 4
    source = jnp.where(upper, jnp.maximum(line - 1, 0), jnp.minimum(line + 1, 3))
    base = jnp.where(upper, 0, LINE - 4)

    def forwards(part):
        return pltpu.make_async_copy(
            received.at[source, UNIT + UNIT * part:2 * UNIT + UNIT * part, :],
            gy_out.at[base + part, 0:UNIT, :],
            sems.at[part],
        )

    @pl.when(edge)
    def _():
        for part in range(4):
            forwards(part).start()

    pieces = [received[other, 5 * UNIT:5 * UNIT + LEVEL3, :] for other in range(4)]
    table = jnp.concatenate(pieces, axis=0)
    total = LINE * LEVEL3
    row = iota((total, SLOTS), 0)
    before = iota((total, SLOTS), 1) < line * LINE + (row >> 4)
    counts = jnp.broadcast_to(box_count[...].astype(jnp.float32), (total, SLOTS))
    start = jnp.sum(jnp.where(before, counts, 0.0), axis=1, keepdims=True).astype(jnp.int32)
    start = jnp.broadcast_to(start, (total, 4 * LEVEL3))
    row = iota((total, 4 * LEVEL3), 0)
    member = start + ((4 * place + (row & 3) - start) & 127)
    wanted = ((member & 511) >> 7) * LEVEL3 + (row & 15)
    choose = jnp.where(iota((total, 4 * LEVEL3), 1) == wanted, 1.0, 0.0).astype(jnp.bfloat16)
    picked[...] = contract(choose, table, (1, 0)).astype(jnp.bfloat16).reshape(LINE, LEVEL3, SLOTS)
    level3 = pltpu.make_async_copy(picked, gy_out.at[:, UNIT:UNIT + LEVEL3, :], sems.at[4])
    level3.start()
    level3.wait()

    @pl.when(edge)
    def _():
        for part in range(4):
            forwards(part).wait()


def forward(gy_buffer, received, box_count):
    whole = pl.BlockSpec(memory_space=pltpu.VMEM)
    return pl.pallas_call(
        forward_kernel,
        out_shape=jax.ShapeDtypeStruct(gy_buffer.shape, gy_buffer.dtype),
        in_specs=[pl.BlockSpec(memory_space=pl.ANY), whole, whole],
        out_specs=pl.BlockSpec(memory_space=pl.ANY),
        scratch_shapes=[pltpu.VMEM((LINE, LEVEL3, SLOTS), jnp.bfloat16), pltpu.SemaphoreType.DMA((5,))],
        input_output_aliases={0: 0},
        compiler_params=VMEM,
        name="forward",
    )(gy_buffer, received, box_count)


def peers(gy_recv, gx_recv, line, place, device):
    out = []
    for step in STEPS:
        there = device + step
        out.append((gy_recv.at[(place + step) & (LINE - 1)], (there >= 0) & (there < 4 * LINE)))
    for bit in (8, 16):
        out.append((gy_recv.at[place ^ bit], None))
    for bit in (1, 2):
        out.append((gx_recv.at[line ^ bit], None))
    return out


def series(u):
    terms = [None, u]
    terms.append(2.0 * u * u - 1.0)
    for degree in range(3, ORDER):
        terms.append(2.0 * u * terms[-1] - terms[-2])
    return terms


def evaluate(coeffs, coords, rows):
    along_x, along_y, along_z = [series(c) for c in coords]

    def line_of(k):
        return jnp.broadcast_to(coeffs[k:k + 1, :], (rows, SLOTS))

    total = None
    for a in range(ORDER):
        plane = None
        for b in range(ORDER):
            base = (a * ORDER + b) * ORDER
            value = line_of(base)
            for c in range(1, ORDER):
                value = value + line_of(base + c) * along_z[c]
            if b:
                value = value * along_y[b]
            plane = value if plane is None else plane + value
        if a:
            plane = plane * along_x[a]
        total = plane if total is None else total + plane
    return total


def far_kernel(mult, gy_recv, gx_recv, far_list, box_count, pos, coarse_coords, operators,
               local_out, eval_out, table, entries, picked, pos_t, coarse_t, level3, both_t):
    line, place, device = position()
    step = pl.program_id(0)

    @pl.when(step == 0)
    def _():
        low, high = [], []
        for message, valid in peers(gy_recv, gx_recv, line, place, device):
            lo = message[0:32, :].astype(jnp.float32)
            hi = message[32:64, :].astype(jnp.float32)
            if valid is not None:
                lo = jnp.where(valid, lo, 0.0)
                hi = jnp.where(valid, hi, 0.0)
            low.append(lo)
            high.append(hi)
        low = jnp.transpose(jnp.concatenate(low, axis=0))
        high = jnp.transpose(jnp.concatenate(high, axis=0))
        table[:, SLOTS:] = jnp.concatenate([low, high[:COEFFS - SLOTS]], axis=0).astype(jnp.bfloat16)
        table[:, :SLOTS] = mult[...]
        listed = far_list[...]
        remote = listed - SLOTS
        compact = SLOTS + 32 * peer_slot(remote >> 5, device) + (remote & 31)
        compact = jnp.where(listed < SLOTS, listed, compact)
        entries[...] = jnp.transpose(compact.astype(jnp.float32)).astype(jnp.int32)
        local_out[...] = jnp.zeros_like(local_out)

    lines = iota((TABLE, SLOTS), 0)
    for pair in range(PER_STEP // 2):
        first = step * PER_STEP + 2 * pair
        hot = []
        for which in range(2):
            wanted = entries[pl.ds(first + which, 1), :]
            hot.append(jnp.where(lines == wanted, 1.0, 0.0).astype(jnp.bfloat16))
        found = contract(table[...], jnp.concatenate(hot, axis=1), (1, 0))
        found = jnp.concatenate([found[:, :SLOTS], found[:, SLOTS:]], axis=0)
        picked[2 * COEFFS * pair:2 * COEFFS * (pair + 1), :] = found.astype(jnp.bfloat16)
    local_out[...] += contract(operators[...], picked[...], (1, 0))

    @pl.when(step == pl.num_programs(0) - 1)
    def _():
        for axis in range(3):
            pos_t[axis] = jnp.transpose(pos[axis])
            coarse_t[axis] = jnp.transpose(coarse_coords[axis])
        before = iota((1, SLOTS), 1) < device
        start = jnp.sum(jnp.where(before, box_count[...].astype(jnp.float32), 0.0), axis=1, keepdims=True)
        start = jnp.broadcast_to(start.astype(jnp.int32), (TABLE, SLOTS))
        pieces = gy_recv[:, UNIT:UNIT + LEVEL3, :].reshape(TABLE, SLOTS)
        pieces = jnp.transpose(pieces.astype(jnp.float32)).astype(jnp.bfloat16)
        row = iota((TABLE, SLOTS), 0)
        member = (row >> 4) * 4 + (row & 3)
        hit = member == ((start + iota((TABLE, SLOTS), 1)) & 127)
        for half in range(2):
            order = jnp.where(hit & (((row >> 2) & 1) == half), 1.0, 0.0).astype(jnp.bfloat16)
            part = contract(pieces, order, (1, 0))
            if half:
                level3[SLOTS:, :] = part[:COEFFS - SLOTS]
            else:
                level3[:SLOTS, :] = part

        rows = 16

        @pl.loop(0, SLOTS // rows)
        def _(index):
            here = pl.ds(pl.multiple_of(index * rows, rows), rows)
            far = evaluate(local_out, [pos_t[axis, here, :] for axis in range(3)], rows)
            coarse = evaluate(level3, [coarse_t[axis, here, :] for axis in range(3)], rows)
            both_t[here, :] = far + coarse

        eval_out[...] = jnp.transpose(both_t[...])


def far_field(mult, gy_recv, gx_recv, far_list, box_count, pos, coarse_coords, operators):
    steps = SLOTS // PER_STEP
    whole = pl.BlockSpec(memory_space=pltpu.VMEM)

    def const(shape):
        return pl.BlockSpec(shape, lambda i: (0,) * len(shape))

    return pl.pallas_call(
        far_kernel,
        grid=(steps,),
        out_shape=(
            jax.ShapeDtypeStruct((COEFFS, SLOTS), jnp.float32),
            jax.ShapeDtypeStruct((SLOTS, SLOTS), jnp.float32),
        ),
        in_specs=[whole] * 7 + [pl.BlockSpec((COEFFS, PER_STEP * COEFFS), lambda i: (0, i))],
        out_specs=(const((COEFFS, SLOTS)), const((SLOTS, SLOTS))),
        scratch_shapes=[
            pltpu.VMEM((COEFFS, TABLE), jnp.bfloat16),
            pltpu.VMEM((SLOTS, SLOTS), jnp.int32),
            pltpu.VMEM((PER_STEP * COEFFS, SLOTS), jnp.bfloat16),
            pltpu.VMEM((3, SLOTS, SLOTS), jnp.float32),
            pltpu.VMEM((3, SLOTS, SLOTS), jnp.float32),
            pltpu.VMEM((COEFFS, SLOTS), jnp.float32),
            pltpu.VMEM((SLOTS, SLOTS), jnp.float32),
        ],
        compiler_params=pltpu.CompilerParams(
            vmem_limit_bytes=56 * 1024 * 1024, dimension_semantics=("arbitrary",)
        ),
        name="far",
    )(mult, gy_recv, gx_recv, far_list, box_count, pos, coarse_coords, operators)


def split(value):
    high = value.astype(jnp.bfloat16).astype(jnp.float32)
    rest = value - high
    middle = rest.astype(jnp.bfloat16).astype(jnp.float32)
    return high, middle, rest - middle


def near_kernel(lists, pos, masked, gy_recv, gx_recv, eval_in, count_row, out,
                source, moves, charge, target, *buffers):
    line, place, device = position()
    row8 = iota((8, SLOTS), 0)

    def stack(x, y, z, norm):
        value = jnp.where((row8 == 0) | (row8 == 5), x, norm)
        value = jnp.where((row8 == 1) | (row8 == 6), y, value)
        return jnp.where((row8 == 2) | (row8 == 7), z, value)

    def put_source(row, x, y, z, q):
        high, middle, low = split(stack(x, y, z, x * x + y * y + z * z))
        g1 = jnp.where(row8 >= 4, 1.0, high)
        g2 = jnp.where(row8 <= 3, middle, jnp.where(row8 == 4, 1.0, high))
        g3 = jnp.where(row8 <= 3, low, jnp.where(row8 == 4, 0.0, middle))
        g5 = jnp.where(row8 <= 4, middle, low)
        source[row, 0:48, :] = jnp.concatenate([g1, g2, g3, g1, g5, g1], axis=0).astype(jnp.bfloat16)
        charge[row] = q

    def put_target(box, x, y, z):
        high, middle, low = split(stack(-2.0 * x, -2.0 * y, -2.0 * z, x * x + y * y + z * z + SOFTENING))
        c1 = jnp.where(row8 == 3, 1.0, high)
        c2 = jnp.where(row8 <= 2, high, 1.0)
        c4 = jnp.where(row8 == 3, 0.0, middle)
        c5 = jnp.where(row8 <= 2, middle, jnp.where(row8 <= 4, 0.0, 1.0))
        c6 = jnp.where(row8 == 3, 0.0, low)
        target[box] = jnp.transpose(jnp.concatenate([c1, c2, c2, c4, c5, c6], axis=0)).astype(jnp.bfloat16)

    @pl.loop(0, SLOTS // 4)
    def _(group):
        for which in range(4):
            box = 4 * group + which
            x, y, z = [jnp.broadcast_to(pos[axis, pl.ds(box, 1), :], (8, SLOTS)) for axis in range(3)]
            put_source(box, x, y, z, jnp.broadcast_to(masked[pl.ds(box, 1), :], (8, SLOTS)))
            put_target(box, x, y, z)

    for j, (message, valid) in enumerate(peers(gy_recv, gx_recv, line, place, device)):
        value = message[64:UNIT, :].astype(jnp.float32)
        for block in range(8):
            rows = [value[8 * field + block:8 * field + block + 1] for field in range(4)]
            put_source(SLOTS + 8 * j + block, *[jnp.broadcast_to(row, (8, SLOTS)) for row in rows])
    none = jnp.zeros((8, SLOTS), jnp.float32)
    put_source(EMPTY, none, none, none, none)

    for code in range(27):
        move = [2.0 * (code // 9 - 1), 2.0 * (code // 3 % 3 - 1), 2.0 * (code % 3 - 1)]
        shift = jnp.full((8, SLOTS), 1.0, jnp.float32)
        for axis in range(3):
            shift = jnp.where(row8 == 5 + axis, move[axis], shift)
        twice = jnp.where(row8 >= 5, 2.0 * shift, shift)
        square = jnp.where(row8 == 4, sum(m * m for m in move), twice)
        moves[code, 0:48, :] = jnp.concatenate([shift, square, twice, shift, twice, shift], axis=0).astype(jnp.bfloat16)

    lag = iota((CHUNK, SLOTS), 1) - iota((CHUNK, SLOTS), 0)

    def prepare(box, rhs, q):
        for n in range(14):
            here = slice(SLOTS * n, SLOTS * n + SLOTS)
            row, move = (lists[n, box], lists[16 + n, box]) if n < 13 else (box, 13)
            rhs[:, here] = source[row, 0:48, :] * moves[move, 0:48, :]
            q[n] = charge[row]

    def compute(box, rhs, q, rows):
        for base in range(0, rows, CHUNK):
            size = min(CHUNK, rows - base)
            mine = target[box, base:base + size, :]
            acc = jnp.zeros((size, SLOTS), jnp.float32)
            for pair in range(7):
                dist = contract(mine, rhs[:, 256 * pair:256 * pair + 256], (1, 0))
                kernel = lax.rsqrt(dist)
                for which in range(2):
                    n = 2 * pair + which
                    part = kernel[:, SLOTS * which:SLOTS * which + SLOTS]
                    if n == 13:
                        part = jnp.where(lag[:size] == base, 0.0, part)
                    acc = acc + part * jnp.concatenate([q[n]] * (size // 8), axis=0)
            out[pl.ds(box, 1), base:base + size] = jnp.sum(jnp.transpose(acc), axis=0, keepdims=True)

    begin = 0
    for chunks in (4, 3, 2, 1):
        end = (lists[14, chunks] + TOGETHER - 1) // TOGETHER

        @pl.loop(begin, end)
        def _(group):
            boxes = [lists[13, TOGETHER * group + which] for which in range(TOGETHER)]
            for which in range(TOGETHER):
                prepare(boxes[which], *buffers[2 * which:2 * which + 2])
            for which in range(TOGETHER):
                compute(boxes[which], *buffers[2 * which:2 * which + 2], 32 * chunks)

        begin = jnp.maximum(begin, end)

    count_col = jnp.transpose(jnp.broadcast_to(count_row[...], (SLOTS, SLOTS)).astype(jnp.float32))
    live = iota((SLOTS, SLOTS), 1).astype(jnp.float32) < count_col
    out[...] = jnp.where(live, out[...] + eval_in[...], 0.0)


def near_field(lists, pos, masked, gy_recv, gx_recv, eval_in, count_row):
    whole = pl.BlockSpec(memory_space=pltpu.VMEM)
    return pl.pallas_call(
        near_kernel,
        out_shape=jax.ShapeDtypeStruct((SLOTS, SLOTS), jnp.float32),
        in_specs=[pl.BlockSpec(memory_space=pltpu.SMEM)] + [whole] * 6,
        out_specs=whole,
        scratch_shapes=[
            pltpu.VMEM((NEAR_ROWS, 64, SLOTS), jnp.bfloat16),
            pltpu.VMEM((27, 64, SLOTS), jnp.bfloat16),
            pltpu.VMEM((NEAR_ROWS, 8, SLOTS), jnp.float32),
            pltpu.VMEM((SLOTS, SLOTS, 48), jnp.bfloat16),
        ] + [
            pltpu.VMEM((48, 14 * SLOTS), jnp.bfloat16),
            pltpu.VMEM((14, 8, SLOTS), jnp.float32),
        ] * TOGETHER,
        compiler_params=VMEM,
        name="near",
    )(lists, pos, masked, gy_recv, gx_recv, eval_in, count_row)


def on_device(
    multipoles,
    operators,
    coarse_local,
    positions,
    charges,
    coarse_coords,
    box_count,
    particle_count,
    expansion_sends,
    far_list,
    block_sends,
    near_list,
    near_offset,
):
    mult = multipoles.T
    pos = jnp.transpose(positions, (1, 0, 2))
    coarse_pos = jnp.transpose(coarse_coords, (1, 0, 2))
    count_row = particle_count.reshape(1, SLOTS)
    box_row = box_count.reshape(1, SLOTS)
    gy_buffer, gx_buffer, masked, lists = pack(
        mult, expansion_sends[0].T, block_sends[0].T, pos, charges, count_row, coarse_local,
        near_list.T, near_offset.T,
    )
    gx_recv = lax.all_to_all(gx_buffer, "gx", 0, 0, tiled=True)
    gy_buffer = forward(gy_buffer, gx_recv, box_row)
    gy_recv = lax.all_to_all(gy_buffer, "gy", 0, 0, tiled=True)
    local_exp, evaluated = far_field(mult, gy_recv, gx_recv, far_list, box_row, pos, coarse_pos, operators)
    potential = near_field(lists, pos, masked, gy_recv, gx_recv, evaluated, count_row)
    return (potential, local_exp)


def solution(mesh):
    both = ("gx", "gy")
    in_specs = (
        P(both, None),
        P(),
        P(both, None),
        P(both, None, None),
        P(both, None),
        P(both, None, None),
        P(),
        P(both),
        P(both, None, None),
        P(both, None),
        P(both, None, None),
        P(both, None),
        P(both, None),
    )
    out_specs = (P(both, None), P(None, both))
    return jax.shard_map(
        on_device, mesh=mesh, in_specs=in_specs, out_specs=out_specs, check_vma=False
    )
```

```python
import functools

import jax
import jax.numpy as jnp
from jax import lax
from jax.experimental import pallas as pl
from jax.experimental.pallas import tpu as pltpu
from jax.sharding import PartitionSpec as P

ORDER = 6
SOFTENING = 0.01
COEFFS = 216
SLOTS = 128
LINE = 32
UNIT = 96
LEVEL3 = 16
TABLE = 512
NEAR_ROWS = 232
EMPTY = 224
STEPS = (-4, -3, -2, -1, 1, 2, 3, 4)
PER_STEP = 32
CHUNK = 128
FIRST, SECOND = 6, 8
ORDER_AT = 2 * FIRST + 4 * SECOND
TOGETHER = 8
VMEM = pltpu.CompilerParams(vmem_limit_bytes=56 * 1024 * 1024)


def iota(shape, dim):
    return lax.broadcasted_iota(jnp.int32, shape, dim)


def position():
    line, place = lax.axis_index("gx"), lax.axis_index("gy")
    return line, place, line * LINE + place


def peer_slot(owner, device):
    delta = owner - device
    cross = owner ^ device
    far = jnp.where(cross == 8, 8, jnp.where(cross == 16, 9, jnp.where(cross == 32, 10, 11)))
    near = jnp.where(delta < 0, delta + 4, delta + 3)
    return jnp.where((delta >= -4) & (delta <= 4), near, far)


def contract(a, b, dims):
    return lax.dot_general(a, b, ((dims[:1], dims[1:]), ((), ())), preferred_element_type=jnp.float32)


def pack_kernel(mult, exp_sends, block_sends, pos, charges, counts, coarse, near_list, near_offset,
                gy_out, gx_out, masked_out, lists_out):
    line, place, device = position()
    lanes = iota((SLOTS, SLOTS), 1)
    count_col = jnp.transpose(jnp.broadcast_to(counts[...], (SLOTS, SLOTS)).astype(jnp.float32))
    masked = jnp.where(lanes.astype(jnp.float32) < count_col, charges[...], 0.0)
    masked_out[...] = masked

    targets = [device + step for step in STEPS] + [device ^ bit for bit in (8, 16, 32, 64)]

    def picks(table):
        rows = table.shape[0]
        values = table[...].astype(jnp.float32)
        lane = iota((rows, SLOTS), 1)
        out = []
        for target in targets:
            column = jnp.sum(jnp.where(lane == target, values, 0.0), axis=1, keepdims=True)
            out.append(jnp.where(column == lane.astype(jnp.float32), 1.0, 0.0))
        return jnp.concatenate(out, axis=0).astype(jnp.bfloat16)

    rows = contract(picks(exp_sends), mult[...], (1, 1))
    low = rows[:, :SLOTS]
    high = jnp.concatenate([rows[:, SLOTS:], jnp.zeros((rows.shape[0], 256 - COEFFS), jnp.float32)], axis=1)
    block_picks = picks(block_sends)
    planes = [pos[0], pos[1], pos[2], masked]
    fields = [contract(block_picks, plane.astype(jnp.bfloat16), (1, 0)) for plane in planes]

    def unit(j):
        parts = [low[32 * j:32 * j + 32], high[32 * j:32 * j + 32]]
        parts += [field[8 * j:8 * j + 8] for field in fields]
        return jnp.concatenate(parts, axis=0).astype(jnp.bfloat16)

    for j, step in enumerate(STEPS):
        value = unit(j)
        there = place + step
        inside = (there >= 0) & (there < LINE)

        @pl.when(inside)
        def _():
            gy_out[there, 0:UNIT, :] = value

        to_line = line + (1 if step > 0 else -1)

        @pl.when(jnp.logical_not(inside) & (to_line >= 0) & (to_line < 4))
        def _():
            part = (there - LINE) if step > 0 else (there + 4)
            gx_out[to_line, pl.ds(pl.multiple_of(UNIT + UNIT * part, UNIT), UNIT), :] = value

    gy_out[place ^ 8, 0:UNIT, :] = unit(8)
    gy_out[place ^ 16, 0:UNIT, :] = unit(9)
    gx_out[line ^ 1, 0:UNIT, :] = unit(10)
    gx_out[line ^ 2, 0:UNIT, :] = unit(11)

    table = coarse[...]
    hi = table.astype(jnp.bfloat16).astype(jnp.float32)
    pieces = []
    for part in (hi, table - hi):
        pieces += [part[:, :SLOTS], jnp.concatenate([part[:, SLOTS:], jnp.zeros((4, 256 - COEFFS), jnp.float32)], axis=1)]
    piece = jnp.concatenate(pieces, axis=0).astype(jnp.bfloat16)
    for other in range(4):
        gx_out[other, 5 * UNIT:5 * UNIT + LEVEL3, :] = piece

    entries = near_list[...]
    remote = entries - SLOTS
    compact = SLOTS + 8 * peer_slot(remote >> 3, device) + (remote & 7)
    row = jnp.where(entries < 0, EMPTY, jnp.where(entries < SLOTS, entries, compact))
    codes = near_offset[...]
    codes = codes + jnp.where(codes >= 13, 1, 0)
    own = jnp.where((entries >= 0) & (entries < SLOTS), 1, 0)
    own_count = jnp.zeros((1, SLOTS), jnp.int32)
    for n in range(13):
        own_count = own_count + own[n:n + 1]
    taken = jnp.minimum(own_count, FIRST - 1)
    place_a, place_b = iota((FIRST, SLOTS), 0), iota((2 * SECOND, SLOTS), 0)
    first_rows = jnp.where(place_a == 0, iota((FIRST, SLOTS), 1), EMPTY)
    first_moves = jnp.full((FIRST, SLOTS), 13, jnp.int32)
    second_rows = jnp.full((2 * SECOND, SLOTS), EMPTY, jnp.int32)
    second_moves = jnp.full((2 * SECOND, SLOTS), 13, jnp.int32)
    seen = jnp.zeros((1, SLOTS), jnp.int32)
    for n in range(13):
        mine = own[n:n + 1] == 1
        early = jnp.where(mine & (seen < FIRST - 1), seen + 1, -1)
        late = jnp.where(mine, seen - (FIRST - 1), own_count - taken + n - seen)
        hit_a, hit_b = place_a == early, place_b == late
        first_rows = jnp.where(hit_a, row[n:n + 1], first_rows)
        first_moves = jnp.where(hit_a, codes[n:n + 1], first_moves)
        second_rows = jnp.where(hit_b, row[n:n + 1], second_rows)
        second_moves = jnp.where(hit_b, codes[n:n + 1], second_moves)
        seen = seen + own[n:n + 1]

    groups = jnp.floor((count_col + 31.0) * (1.0 / 32.0))
    more = jnp.transpose(jnp.broadcast_to(13 - taken, (SLOTS, SLOTS)).astype(jnp.float32))
    index = iota((SLOTS, SLOTS), 0)
    orders = []
    for groups in (groups, jnp.where(more > SECOND, groups, 0.0)):
        other = jnp.transpose(groups)
        ahead = (groups > other) | ((groups == other) & (index < lanes))
        rank = jnp.sum(jnp.where(ahead, 1.0, 0.0), axis=0, keepdims=True)
        rank = jnp.transpose(jnp.broadcast_to(rank, (SLOTS, SLOTS)))
        orders.append(jnp.sum(jnp.where(rank == lanes.astype(jnp.float32), index.astype(jnp.float32), 0.0), axis=0, keepdims=True))
        orders.append(jnp.sum(jnp.where(groups >= lanes.astype(jnp.float32), 1.0, 0.0), axis=0, keepdims=True))
    plan = [part.astype(jnp.float32) for part in (first_rows, first_moves, second_rows, second_moves)]
    plan.append(jnp.concatenate(orders + [jnp.zeros((SLOTS - ORDER_AT - 4, SLOTS), jnp.float32)], axis=0))
    lists_out[...] = jnp.transpose(jnp.concatenate(plan, axis=0)).astype(jnp.int32)


def pack(mult, exp_sends, block_sends, pos, charges, counts, coarse, near_list, near_offset):
    return pl.pallas_call(
        pack_kernel,
        out_shape=(
            jax.ShapeDtypeStruct((LINE, UNIT + LEVEL3, SLOTS), jnp.bfloat16),
            jax.ShapeDtypeStruct((4, 5 * UNIT + LEVEL3, SLOTS), jnp.bfloat16),
            jax.ShapeDtypeStruct((SLOTS, SLOTS), jnp.float32),
            jax.ShapeDtypeStruct((SLOTS, SLOTS), jnp.int32),
        ),
        compiler_params=VMEM,
        name="pack",
    )(mult, exp_sends, block_sends, pos, charges, counts, coarse, near_list, near_offset)


def forward_kernel(gy_in, received, box_count, gy_out, picked, sems):
    line, place, device = position()
    edge = (place >= LINE - 4) | (place < 4)
    upper = place >= LINE - 4
    source = jnp.where(upper, jnp.maximum(line - 1, 0), jnp.minimum(line + 1, 3))
    base = jnp.where(upper, 0, LINE - 4)

    def forwards(part):
        return pltpu.make_async_copy(
            received.at[source, UNIT + UNIT * part:2 * UNIT + UNIT * part, :],
            gy_out.at[base + part, 0:UNIT, :],
            sems.at[part],
        )

    @pl.when(edge)
    def _():
        for part in range(4):
            forwards(part).start()

    pieces = [received[other, 5 * UNIT:5 * UNIT + LEVEL3, :] for other in range(4)]
    table = jnp.concatenate(pieces, axis=0)
    total = LINE * LEVEL3
    row = iota((total, SLOTS), 0)
    before = iota((total, SLOTS), 1) < line * LINE + (row >> 4)
    counts = jnp.broadcast_to(box_count[...].astype(jnp.float32), (total, SLOTS))
    start = jnp.sum(jnp.where(before, counts, 0.0), axis=1, keepdims=True).astype(jnp.int32)
    start = jnp.broadcast_to(start, (total, 4 * LEVEL3))
    row = iota((total, 4 * LEVEL3), 0)
    member = start + ((4 * place + (row & 3) - start) & 127)
    wanted = ((member & 511) >> 7) * LEVEL3 + (row & 15)
    choose = jnp.where(iota((total, 4 * LEVEL3), 1) == wanted, 1.0, 0.0).astype(jnp.bfloat16)
    picked[...] = contract(choose, table, (1, 0)).astype(jnp.bfloat16).reshape(LINE, LEVEL3, SLOTS)
    level3 = pltpu.make_async_copy(picked, gy_out.at[:, UNIT:UNIT + LEVEL3, :], sems.at[4])
    level3.start()
    level3.wait()

    @pl.when(edge)
    def _():
        for part in range(4):
            forwards(part).wait()


def forward(gy_buffer, received, box_count):
    whole = pl.BlockSpec(memory_space=pltpu.VMEM)
    return pl.pallas_call(
        forward_kernel,
        out_shape=jax.ShapeDtypeStruct(gy_buffer.shape, gy_buffer.dtype),
        in_specs=[pl.BlockSpec(memory_space=pl.ANY), whole, whole],
        out_specs=pl.BlockSpec(memory_space=pl.ANY),
        scratch_shapes=[pltpu.VMEM((LINE, LEVEL3, SLOTS), jnp.bfloat16), pltpu.SemaphoreType.DMA((5,))],
        input_output_aliases={0: 0},
        compiler_params=VMEM,
        name="forward",
    )(gy_buffer, received, box_count)


def peers(gy_recv, gx_recv, line, place, device):
    out = []
    for step in STEPS:
        there = device + step
        out.append((gy_recv.at[(place + step) & (LINE - 1)], (there >= 0) & (there < 4 * LINE)))
    for bit in (8, 16):
        out.append((gy_recv.at[place ^ bit], None))
    for bit in (1, 2):
        out.append((gx_recv.at[line ^ bit], None))
    return out


def series(u):
    terms = [None, u]
    terms.append(2.0 * u * u - 1.0)
    for degree in range(3, ORDER):
        terms.append(2.0 * u * terms[-1] - terms[-2])
    return terms


def evaluate(coeffs, coords, rows):
    along_x, along_y, along_z = [series(c) for c in coords]

    def line_of(k):
        return jnp.broadcast_to(coeffs[k:k + 1, :], (rows, SLOTS))

    total = None
    for a in range(ORDER):
        plane = None
        for b in range(ORDER):
            base = (a * ORDER + b) * ORDER
            value = line_of(base)
            for c in range(1, ORDER):
                value = value + line_of(base + c) * along_z[c]
            if b:
                value = value * along_y[b]
            plane = value if plane is None else plane + value
        if a:
            plane = plane * along_x[a]
        total = plane if total is None else total + plane
    return total


def far_kernel(mult, gy_recv, gx_recv, far_list, box_count, pos, coarse_coords, operators,
               local_out, eval_out, table, entries, picked, pos_t, coarse_t, level3, both_t):
    line, place, device = position()
    step = pl.program_id(0)

    @pl.when(step == 0)
    def _():
        low, high = [], []
        for message, valid in peers(gy_recv, gx_recv, line, place, device):
            lo = message[0:32, :].astype(jnp.float32)
            hi = message[32:64, :].astype(jnp.float32)
            if valid is not None:
                lo = jnp.where(valid, lo, 0.0)
                hi = jnp.where(valid, hi, 0.0)
            low.append(lo)
            high.append(hi)
        low = jnp.transpose(jnp.concatenate(low, axis=0))
        high = jnp.transpose(jnp.concatenate(high, axis=0))
        table[:, SLOTS:] = jnp.concatenate([low, high[:COEFFS - SLOTS]], axis=0).astype(jnp.bfloat16)
        table[:, :SLOTS] = mult[...]
        listed = far_list[...]
        remote = listed - SLOTS
        compact = SLOTS + 32 * peer_slot(remote >> 5, device) + (remote & 31)
        compact = jnp.where(listed < SLOTS, listed, compact)
        entries[...] = jnp.transpose(compact.astype(jnp.float32)).astype(jnp.int32)
        local_out[...] = jnp.zeros_like(local_out)
        for axis in range(3):
            pos_t[axis] = jnp.transpose(pos[axis])
            coarse_t[axis] = jnp.transpose(coarse_coords[axis])
        before = iota((1, SLOTS), 1) < device
        start = jnp.sum(jnp.where(before, box_count[...].astype(jnp.float32), 0.0), axis=1, keepdims=True)
        start = jnp.broadcast_to(start.astype(jnp.int32), (TABLE, SLOTS))
        pieces = gy_recv[:, UNIT:UNIT + LEVEL3, :].reshape(TABLE, SLOTS)
        pieces = jnp.transpose(pieces.astype(jnp.float32)).astype(jnp.bfloat16)
        row = iota((TABLE, SLOTS), 0)
        member = (row >> 4) * 4 + (row & 3)
        hit = member == ((start + iota((TABLE, SLOTS), 1)) & 127)
        for half in range(2):
            order = jnp.where(hit & (((row >> 2) & 1) == half), 1.0, 0.0).astype(jnp.bfloat16)
            part = contract(pieces, order, (1, 0))
            if half:
                level3[SLOTS:, :] = part[:COEFFS - SLOTS]
            else:
                level3[:SLOTS, :] = part

    lines = iota((TABLE, SLOTS), 0).astype(jnp.int16)
    one, zero = jnp.ones((), jnp.bfloat16), jnp.zeros((), jnp.bfloat16)
    for pair in range(PER_STEP // 2):
        first = step * PER_STEP + 2 * pair
        hot = []
        for which in range(2):
            wanted = jnp.broadcast_to(entries[pl.ds(first + which, 1), :], (16, SLOTS)).astype(jnp.int16)
            wanted = jnp.concatenate([wanted] * (TABLE // 16), axis=0)
            hot.append(jnp.where(lines == wanted, one, zero))
        found = contract(table[...], jnp.concatenate(hot, axis=1), (1, 0))
        found = jnp.concatenate([found[:, :SLOTS], found[:, SLOTS:]], axis=0)
        picked[2 * COEFFS * pair:2 * COEFFS * (pair + 1), :] = found.astype(jnp.bfloat16)
    local_out[...] += contract(operators[...], picked[...], (1, 0))
    rows = 16
    for part in range(PER_STEP // rows):
        here = pl.ds(pl.multiple_of(step * PER_STEP + part * rows, rows), rows)
        both_t[here, :] = evaluate(level3, [coarse_t[axis, here, :] for axis in range(3)], rows)

    @pl.when(step == pl.num_programs(0) - 1)
    def _():
        @pl.loop(0, SLOTS // rows)
        def _(index):
            here = pl.ds(pl.multiple_of(index * rows, rows), rows)
            far = evaluate(local_out, [pos_t[axis, here, :] for axis in range(3)], rows)
            both_t[here, :] = both_t[here, :] + far

        eval_out[...] = jnp.transpose(both_t[...])


def far_field(mult, gy_recv, gx_recv, far_list, box_count, pos, coarse_coords, operators):
    steps = SLOTS // PER_STEP
    whole = pl.BlockSpec(memory_space=pltpu.VMEM)

    def const(shape):
        return pl.BlockSpec(shape, lambda i: (0,) * len(shape))

    return pl.pallas_call(
        far_kernel,
        grid=(steps,),
        out_shape=(
            jax.ShapeDtypeStruct((COEFFS, SLOTS), jnp.float32),
            jax.ShapeDtypeStruct((SLOTS, SLOTS), jnp.float32),
        ),
        in_specs=[whole] * 7 + [pl.BlockSpec((COEFFS, PER_STEP * COEFFS), lambda i: (0, i))],
        out_specs=(const((COEFFS, SLOTS)), const((SLOTS, SLOTS))),
        scratch_shapes=[
            pltpu.VMEM((COEFFS, TABLE), jnp.bfloat16),
            pltpu.VMEM((SLOTS, SLOTS), jnp.int32),
            pltpu.VMEM((PER_STEP * COEFFS, SLOTS), jnp.bfloat16),
            pltpu.VMEM((3, SLOTS, SLOTS), jnp.float32),
            pltpu.VMEM((3, SLOTS, SLOTS), jnp.float32),
            pltpu.VMEM((COEFFS, SLOTS), jnp.float32),
            pltpu.VMEM((SLOTS, SLOTS), jnp.float32),
        ],
        compiler_params=pltpu.CompilerParams(
            vmem_limit_bytes=56 * 1024 * 1024, dimension_semantics=("arbitrary",)
        ),
        name="far",
    )(mult, gy_recv, gx_recv, far_list, box_count, pos, coarse_coords, operators)


def split(value):
    high = value.astype(jnp.bfloat16).astype(jnp.float32)
    rest = value - high
    middle = rest.astype(jnp.bfloat16).astype(jnp.float32)
    return high, middle, rest - middle


class Near:
    scratch = [
        pltpu.VMEM((NEAR_ROWS, 64, SLOTS), jnp.bfloat16),
        pltpu.VMEM((27, 64, SLOTS), jnp.bfloat16),
        pltpu.VMEM((NEAR_ROWS, 8, SLOTS), jnp.float32),
        pltpu.VMEM((SLOTS, SLOTS, 48), jnp.bfloat16),
    ] + [
        pltpu.VMEM((48, max(FIRST, SECOND) * SLOTS), jnp.bfloat16),
        pltpu.VMEM((max(FIRST, SECOND), 8, SLOTS), jnp.float32),
    ] * TOGETHER

    def __init__(self, lists, pos, masked, out, source, moves, charge, target, *buffers):
        self.lists, self.pos, self.masked, self.out = lists, pos, masked, out
        self.source, self.moves, self.charge, self.target, self.buffers = source, moves, charge, target, buffers
        self.row8 = iota((8, SLOTS), 0)
        self.lag = iota((CHUNK, SLOTS), 1) - iota((CHUNK, SLOTS), 0)

    def stack(self, x, y, z, norm):
        value = jnp.where((self.row8 == 0) | (self.row8 == 5), x, norm)
        value = jnp.where((self.row8 == 1) | (self.row8 == 6), y, value)
        return jnp.where((self.row8 == 2) | (self.row8 == 7), z, value)

    def put_source(self, row, x, y, z, q):
        row8 = self.row8
        high, middle, low = split(self.stack(x, y, z, x * x + y * y + z * z))
        g1 = jnp.where(row8 >= 4, 1.0, high)
        g2 = jnp.where(row8 <= 3, middle, jnp.where(row8 == 4, 1.0, high))
        g3 = jnp.where(row8 <= 3, low, jnp.where(row8 == 4, 0.0, middle))
        g5 = jnp.where(row8 <= 4, middle, low)
        self.source[row, 0:48, :] = jnp.concatenate([g1, g2, g3, g1, g5, g1], axis=0).astype(jnp.bfloat16)
        self.charge[row] = q

    def put_target(self, box, x, y, z):
        row8 = self.row8
        norm = x * x + y * y + z * z + SOFTENING
        high, middle, low = split(self.stack(-2.0 * x, -2.0 * y, -2.0 * z, norm))
        c1 = jnp.where(row8 == 3, 1.0, high)
        c2 = jnp.where(row8 <= 2, high, 1.0)
        c4 = jnp.where(row8 == 3, 0.0, middle)
        c5 = jnp.where(row8 <= 2, middle, jnp.where(row8 <= 4, 0.0, 1.0))
        c6 = jnp.where(row8 == 3, 0.0, low)
        columns = jnp.concatenate([c1, c2, c2, c4, c5, c6], axis=0)
        self.target[box] = jnp.transpose(columns).astype(jnp.bfloat16)

    def tables(self):
        @pl.loop(0, SLOTS // 16)
        def _(group):
            for which in range(16):
                box = 16 * group + which
                here = pl.ds(box, 1)
                x, y, z = [jnp.broadcast_to(self.pos[axis, here, :], (8, SLOTS)) for axis in range(3)]
                self.put_source(box, x, y, z, jnp.broadcast_to(self.masked[here, :], (8, SLOTS)))
                self.put_target(box, x, y, z)

        none = jnp.zeros((8, SLOTS), jnp.float32)
        self.put_source(EMPTY, none, none, none, none)
        row8 = self.row8
        for code in range(27):
            move = [2.0 * (code // 9 - 1), 2.0 * (code // 3 % 3 - 1), 2.0 * (code % 3 - 1)]
            shift = jnp.full((8, SLOTS), 1.0, jnp.float32)
            for axis in range(3):
                shift = jnp.where(row8 == 5 + axis, move[axis], shift)
            twice = jnp.where(row8 >= 5, 2.0 * shift, shift)
            square = jnp.where(row8 == 4, sum(m * m for m in move), twice)
            groups = jnp.concatenate([shift, square, twice, shift, twice, shift], axis=0)
            self.moves[code, 0:48, :] = groups.astype(jnp.bfloat16)

    def remote(self, messages):
        for j, (message, valid) in enumerate(messages):
            value = message[64:UNIT, :].astype(jnp.float32)
            for block in range(8):
                rows = [value[8 * field + block:8 * field + block + 1] for field in range(4)]
                self.put_source(SLOTS + 8 * j + block, *[jnp.broadcast_to(row, (8, SLOTS)) for row in rows])

    def prepare(self, box, rows_at, moves_at, width, rhs, q):
        for n in range(width):
            row, move = self.lists[box, rows_at + n], self.lists[box, moves_at + n]
            rhs[:, SLOTS * n:SLOTS * n + SLOTS] = self.source[row, 0:48, :] * self.moves[move, 0:48, :]
            q[n] = self.charge[row]

    def compute(self, box, width, rhs, q, rows, first):
        for base in range(0, rows, CHUNK):
            size = min(CHUNK, rows - base)
            mine = self.target[box, base:base + size, :]
            acc = jnp.zeros((size, SLOTS), jnp.float32)
            for pair in range(width // 2):
                dist = contract(mine, rhs[:, 256 * pair:256 * pair + 256], (1, 0))
                kernel = lax.rsqrt(dist)
                for which in range(2):
                    n = 2 * pair + which
                    part = kernel[:, SLOTS * which:SLOTS * which + SLOTS]
                    if first and n == 0:
                        part = jnp.where(self.lag[:size] == base, 0.0, part)
                    acc = acc + part * jnp.concatenate([q[n]] * (size // 8), axis=0)
            value = jnp.sum(jnp.transpose(acc), axis=0, keepdims=True)
            here = pl.ds(box, 1), slice(base, base + size)
            self.out[here] = value if first else self.out[here] + value

    def run(self, rows_at, moves_at, width, order, first):
        begin = 0
        for chunks in (4, 3, 2, 1):
            end = (self.lists[chunks, order + 1] + TOGETHER - 1) // TOGETHER

            @pl.loop(begin, end)
            def _(group):
                boxes = [self.lists[TOGETHER * group + which, order] for which in range(TOGETHER)]
                for which in range(TOGETHER):
                    self.prepare(boxes[which], rows_at, moves_at, width, *self.buffers[2 * which:2 * which + 2])
                for which in range(TOGETHER):
                    self.compute(boxes[which], width, *self.buffers[2 * which:2 * which + 2], 32 * chunks, first)

            begin = jnp.maximum(begin, end)


def near_own_kernel(lists, pos, masked, after, out, *scratch):
    near = Near(lists, pos, masked, out, *scratch)
    near.tables()
    near.run(0, FIRST, FIRST, ORDER_AT, True)


def near_kernel(lists, pos, masked, gy_recv, gx_recv, near_in, eval_in, count_row, out, *scratch):
    near = Near(lists, pos, masked, out, *scratch)
    near.tables()
    near.remote(peers(gy_recv, gx_recv, *position()))
    out[...] = near_in[...] + eval_in[...]

    for part in range(2):
        rows_at = 2 * FIRST + SECOND * part
        near.run(rows_at, rows_at + 2 * SECOND, SECOND, ORDER_AT + 2 * part, False)

    count_col = jnp.transpose(jnp.broadcast_to(count_row[...], (SLOTS, SLOTS)).astype(jnp.float32))
    live = iota((SLOTS, SLOTS), 1).astype(jnp.float32) < count_col
    out[...] = jnp.where(live, out[...], 0.0)


def near_own(lists, pos, masked, after):
    whole = pl.BlockSpec(memory_space=pltpu.VMEM)
    return pl.pallas_call(
        near_own_kernel,
        out_shape=jax.ShapeDtypeStruct((SLOTS, SLOTS), jnp.float32),
        in_specs=[pl.BlockSpec(memory_space=pltpu.SMEM), whole, whole, pl.BlockSpec(memory_space=pl.ANY)],
        out_specs=whole,
        scratch_shapes=Near.scratch,
        compiler_params=VMEM,
        cost_estimate=pl.CostEstimate(flops=10**9, bytes_accessed=6 * 10**7, transcendentals=2 * 10**7),
        name="near_own",
    )(lists, pos, masked, after)


def near_field(lists, pos, masked, gy_recv, gx_recv, near_in, eval_in, count_row):
    whole = pl.BlockSpec(memory_space=pltpu.VMEM)
    return pl.pallas_call(
        near_kernel,
        out_shape=jax.ShapeDtypeStruct((SLOTS, SLOTS), jnp.float32),
        in_specs=[pl.BlockSpec(memory_space=pltpu.SMEM)] + [whole] * 7,
        out_specs=whole,
        scratch_shapes=Near.scratch,
        compiler_params=VMEM,
        name="near",
    )(lists, pos, masked, gy_recv, gx_recv, near_in, eval_in, count_row)


def on_device(
    multipoles,
    operators,
    coarse_local,
    positions,
    charges,
    coarse_coords,
    box_count,
    particle_count,
    expansion_sends,
    far_list,
    block_sends,
    near_list,
    near_offset,
):
    mult = multipoles.T
    pos = jnp.transpose(positions, (1, 0, 2))
    coarse_pos = jnp.transpose(coarse_coords, (1, 0, 2))
    count_row = particle_count.reshape(1, SLOTS)
    box_row = box_count.reshape(1, SLOTS)
    gy_buffer, gx_buffer, masked, lists = pack(
        mult, expansion_sends[0].T, block_sends[0].T, pos, charges, count_row, coarse_local,
        near_list.T, near_offset.T,
    )
    gx_recv = lax.all_to_all(gx_buffer, "gx", 0, 0, tiled=True)
    gy_buffer = forward(gy_buffer, gx_recv, box_row)
    near = near_own(lists, pos, masked, gy_buffer)
    gy_recv = lax.all_to_all(gy_buffer, "gy", 0, 0, tiled=True)
    local_exp, evaluated = far_field(mult, gy_recv, gx_recv, far_list, box_row, pos, coarse_pos, operators)
    potential = near_field(lists, pos, masked, gy_recv, gx_recv, near, evaluated, count_row)
    return (potential, local_exp)


def solution(mesh):
    both = ("gx", "gy")
    in_specs = (
        P(both, None),
        P(),
        P(both, None),
        P(both, None, None),
        P(both, None),
        P(both, None, None),
        P(),
        P(both),
        P(both, None, None),
        P(both, None),
        P(both, None, None),
        P(both, None),
        P(both, None),
    )
    out_specs = (P(both, None), P(None, both))
    return jax.shard_map(
        on_device, mesh=mesh, in_specs=in_specs, out_specs=out_specs, check_vma=False
    )
```

```python
import functools

import jax
import jax.numpy as jnp
from jax import lax
from jax.experimental import pallas as pl
from jax.experimental.pallas import tpu as pltpu
from jax.sharding import PartitionSpec as P

ORDER = 6
SOFTENING = 0.01
COEFFS = 216
SLOTS = 128
LINE = 32
UNIT = 96
LEVEL3 = 16
TABLE = 512
NEAR_ROWS = 232
EMPTY = 224
STEPS = (-4, -3, -2, -1, 1, 2, 3, 4)
PER_STEP = 32
CHUNK = 128
FIRST, SECOND = 6, 8
ORDER_AT = 2 * FIRST + 4 * SECOND
TOGETHER = 16
VMEM = pltpu.CompilerParams(vmem_limit_bytes=56 * 1024 * 1024)


def iota(shape, dim):
    return lax.broadcasted_iota(jnp.int32, shape, dim)


def position():
    line, place = lax.axis_index("gx"), lax.axis_index("gy")
    return line, place, line * LINE + place


def peer_slot(owner, device):
    delta = owner - device
    cross = owner ^ device
    far = jnp.where(cross == 8, 8, jnp.where(cross == 16, 9, jnp.where(cross == 32, 10, 11)))
    near = jnp.where(delta < 0, delta + 4, delta + 3)
    return jnp.where((delta >= -4) & (delta <= 4), near, far)


def contract(a, b, dims):
    return lax.dot_general(a, b, ((dims[:1], dims[1:]), ((), ())), preferred_element_type=jnp.float32)


def pack_kernel(mult, exp_sends, block_sends, pos, charges, counts, coarse, near_list, near_offset,
                gy_out, gx_out, masked_out, lists_out):
    line, place, device = position()
    lanes = iota((SLOTS, SLOTS), 1)
    count_col = jnp.transpose(jnp.broadcast_to(counts[...], (SLOTS, SLOTS)).astype(jnp.float32))
    masked = jnp.where(lanes.astype(jnp.float32) < count_col, charges[...], 0.0)
    masked_out[...] = masked

    targets = [device + step for step in STEPS] + [device ^ bit for bit in (8, 16, 32, 64)]

    def picks(table):
        rows = table.shape[0]
        values = table[...].astype(jnp.float32)
        lane = iota((rows, SLOTS), 1)
        out = []
        for target in targets:
            column = jnp.sum(jnp.where(lane == target, values, 0.0), axis=1, keepdims=True)
            out.append(jnp.where(column == lane.astype(jnp.float32), 1.0, 0.0))
        return jnp.concatenate(out, axis=0).astype(jnp.bfloat16)

    rows = contract(picks(exp_sends), mult[...], (1, 1))
    low = rows[:, :SLOTS]
    high = jnp.concatenate([rows[:, SLOTS:], jnp.zeros((rows.shape[0], 256 - COEFFS), jnp.float32)], axis=1)
    block_picks = picks(block_sends)
    planes = [pos[0], pos[1], pos[2], masked]
    fields = [contract(block_picks, plane.astype(jnp.bfloat16), (1, 0)) for plane in planes]

    def unit(j):
        parts = [low[32 * j:32 * j + 32], high[32 * j:32 * j + 32]]
        parts += [field[8 * j:8 * j + 8] for field in fields]
        return jnp.concatenate(parts, axis=0).astype(jnp.bfloat16)

    for j, step in enumerate(STEPS):
        value = unit(j)
        there = place + step
        inside = (there >= 0) & (there < LINE)

        @pl.when(inside)
        def _():
            gy_out[there, 0:UNIT, :] = value

        to_line = line + (1 if step > 0 else -1)

        @pl.when(jnp.logical_not(inside) & (to_line >= 0) & (to_line < 4))
        def _():
            part = (there - LINE) if step > 0 else (there + 4)
            gx_out[to_line, pl.ds(pl.multiple_of(UNIT + UNIT * part, UNIT), UNIT), :] = value

    gy_out[place ^ 8, 0:UNIT, :] = unit(8)
    gy_out[place ^ 16, 0:UNIT, :] = unit(9)
    gx_out[line ^ 1, 0:UNIT, :] = unit(10)
    gx_out[line ^ 2, 0:UNIT, :] = unit(11)

    table = coarse[...]
    hi = table.astype(jnp.bfloat16).astype(jnp.float32)
    pieces = []
    for part in (hi, table - hi):
        pieces += [part[:, :SLOTS], jnp.concatenate([part[:, SLOTS:], jnp.zeros((4, 256 - COEFFS), jnp.float32)], axis=1)]
    piece = jnp.concatenate(pieces, axis=0).astype(jnp.bfloat16)
    for other in range(4):
        gx_out[other, 5 * UNIT:5 * UNIT + LEVEL3, :] = piece

    entries = near_list[...]
    remote = entries - SLOTS
    compact = SLOTS + 8 * peer_slot(remote >> 3, device) + (remote & 7)
    row = jnp.where(entries < 0, EMPTY, jnp.where(entries < SLOTS, entries, compact))
    codes = near_offset[...]
    codes = codes + jnp.where(codes >= 13, 1, 0)
    own = jnp.where((entries >= 0) & (entries < SLOTS), 1, 0)
    own_count = jnp.zeros((1, SLOTS), jnp.int32)
    for n in range(13):
        own_count = own_count + own[n:n + 1]
    taken = jnp.minimum(own_count, FIRST - 1)
    place_a, place_b = iota((FIRST, SLOTS), 0), iota((2 * SECOND, SLOTS), 0)
    first_rows = jnp.where(place_a == 0, iota((FIRST, SLOTS), 1), EMPTY)
    first_moves = jnp.full((FIRST, SLOTS), 13, jnp.int32)
    second_rows = jnp.full((2 * SECOND, SLOTS), EMPTY, jnp.int32)
    second_moves = jnp.full((2 * SECOND, SLOTS), 13, jnp.int32)
    seen = jnp.zeros((1, SLOTS), jnp.int32)
    for n in range(13):
        mine = own[n:n + 1] == 1
        early = jnp.where(mine & (seen < FIRST - 1), seen + 1, -1)
        late = jnp.where(mine, seen - (FIRST - 1), own_count - taken + n - seen)
        hit_a, hit_b = place_a == early, place_b == late
        first_rows = jnp.where(hit_a, row[n:n + 1], first_rows)
        first_moves = jnp.where(hit_a, codes[n:n + 1], first_moves)
        second_rows = jnp.where(hit_b, row[n:n + 1], second_rows)
        second_moves = jnp.where(hit_b, codes[n:n + 1], second_moves)
        seen = seen + own[n:n + 1]

    groups = jnp.floor((count_col + 31.0) * (1.0 / 32.0))
    more = jnp.transpose(jnp.broadcast_to(13 - taken, (SLOTS, SLOTS)).astype(jnp.float32))
    index = iota((SLOTS, SLOTS), 0)
    orders = []
    for groups in (groups, jnp.where(more > SECOND, groups, 0.0)):
        other = jnp.transpose(groups)
        ahead = (groups > other) | ((groups == other) & (index < lanes))
        rank = jnp.sum(jnp.where(ahead, 1.0, 0.0), axis=0, keepdims=True)
        rank = jnp.transpose(jnp.broadcast_to(rank, (SLOTS, SLOTS)))
        orders.append(jnp.sum(jnp.where(rank == lanes.astype(jnp.float32), index.astype(jnp.float32), 0.0), axis=0, keepdims=True))
        orders.append(jnp.sum(jnp.where(groups >= lanes.astype(jnp.float32), 1.0, 0.0), axis=0, keepdims=True))
    plan = [part.astype(jnp.float32) for part in (first_rows, first_moves, second_rows, second_moves)]
    plan.append(jnp.concatenate(orders + [jnp.zeros((SLOTS - ORDER_AT - 4, SLOTS), jnp.float32)], axis=0))
    lists_out[...] = jnp.transpose(jnp.concatenate(plan, axis=0)).astype(jnp.int32)


def pack(mult, exp_sends, block_sends, pos, charges, counts, coarse, near_list, near_offset):
    return pl.pallas_call(
        pack_kernel,
        out_shape=(
            jax.ShapeDtypeStruct((LINE, UNIT + LEVEL3, SLOTS), jnp.bfloat16),
            jax.ShapeDtypeStruct((4, 5 * UNIT + LEVEL3, SLOTS), jnp.bfloat16),
            jax.ShapeDtypeStruct((SLOTS, SLOTS), jnp.float32),
            jax.ShapeDtypeStruct((SLOTS, SLOTS), jnp.int32),
        ),
        compiler_params=VMEM,
        name="pack",
    )(mult, exp_sends, block_sends, pos, charges, counts, coarse, near_list, near_offset)


def forward_kernel(gy_in, received, box_count, gy_out, picked, sems):
    line, place, device = position()
    edge = (place >= LINE - 4) | (place < 4)
    upper = place >= LINE - 4
    source = jnp.where(upper, jnp.maximum(line - 1, 0), jnp.minimum(line + 1, 3))
    base = jnp.where(upper, 0, LINE - 4)

    def forwards(part):
        return pltpu.make_async_copy(
            received.at[source, UNIT + UNIT * part:2 * UNIT + UNIT * part, :],
            gy_out.at[base + part, 0:UNIT, :],
            sems.at[part],
        )

    @pl.when(edge)
    def _():
        for part in range(4):
            forwards(part).start()

    pieces = [received[other, 5 * UNIT:5 * UNIT + LEVEL3, :] for other in range(4)]
    table = jnp.concatenate(pieces, axis=0)
    total = LINE * LEVEL3
    row = iota((total, SLOTS), 0)
    before = iota((total, SLOTS), 1) < line * LINE + (row >> 4)
    counts = jnp.broadcast_to(box_count[...].astype(jnp.float32), (total, SLOTS))
    start = jnp.sum(jnp.where(before, counts, 0.0), axis=1, keepdims=True).astype(jnp.int32)
    start = jnp.broadcast_to(start, (total, 4 * LEVEL3))
    row = iota((total, 4 * LEVEL3), 0)
    member = start + ((4 * place + (row & 3) - start) & 127)
    wanted = ((member & 511) >> 7) * LEVEL3 + (row & 15)
    choose = jnp.where(iota((total, 4 * LEVEL3), 1) == wanted, 1.0, 0.0).astype(jnp.bfloat16)
    picked[...] = contract(choose, table, (1, 0)).astype(jnp.bfloat16).reshape(LINE, LEVEL3, SLOTS)
    level3 = pltpu.make_async_copy(picked, gy_out.at[:, UNIT:UNIT + LEVEL3, :], sems.at[4])
    level3.start()
    level3.wait()

    @pl.when(edge)
    def _():
        for part in range(4):
            forwards(part).wait()


def forward(gy_buffer, received, box_count):
    whole = pl.BlockSpec(memory_space=pltpu.VMEM)
    return pl.pallas_call(
        forward_kernel,
        out_shape=jax.ShapeDtypeStruct(gy_buffer.shape, gy_buffer.dtype),
        in_specs=[pl.BlockSpec(memory_space=pl.ANY), whole, whole],
        out_specs=pl.BlockSpec(memory_space=pl.ANY),
        scratch_shapes=[pltpu.VMEM((LINE, LEVEL3, SLOTS), jnp.bfloat16), pltpu.SemaphoreType.DMA((5,))],
        input_output_aliases={0: 0},
        compiler_params=VMEM,
        name="forward",
    )(gy_buffer, received, box_count)


def peers(gy_recv, gx_recv, line, place, device):
    out = []
    for step in STEPS:
        there = device + step
        out.append((gy_recv.at[(place + step) & (LINE - 1)], (there >= 0) & (there < 4 * LINE)))
    for bit in (8, 16):
        out.append((gy_recv.at[place ^ bit], None))
    for bit in (1, 2):
        out.append((gx_recv.at[line ^ bit], None))
    return out


def series(u):
    terms = [None, u]
    terms.append(2.0 * u * u - 1.0)
    for degree in range(3, ORDER):
        terms.append(2.0 * u * terms[-1] - terms[-2])
    return terms


def evaluate(coeffs, coords, rows):
    along_x, along_y, along_z = [series(c) for c in coords]

    def line_of(k):
        return jnp.broadcast_to(coeffs[k:k + 1, :], (rows, SLOTS))

    total = None
    for a in range(ORDER):
        plane = None
        for b in range(ORDER):
            base = (a * ORDER + b) * ORDER
            value = line_of(base)
            for c in range(1, ORDER):
                value = value + line_of(base + c) * along_z[c]
            if b:
                value = value * along_y[b]
            plane = value if plane is None else plane + value
        if a:
            plane = plane * along_x[a]
        total = plane if total is None else total + plane
    return total


def far_kernel(mult, gy_recv, gx_recv, far_list, box_count, pos, coarse_coords, operators,
               local_out, eval_out, table, entries, picked, pos_t, coarse_t, level3, both_t):
    line, place, device = position()
    step = pl.program_id(0)

    @pl.when(step == 0)
    def _():
        low, high = [], []
        for message, valid in peers(gy_recv, gx_recv, line, place, device):
            lo = message[0:32, :].astype(jnp.float32)
            hi = message[32:64, :].astype(jnp.float32)
            if valid is not None:
                lo = jnp.where(valid, lo, 0.0)
                hi = jnp.where(valid, hi, 0.0)
            low.append(lo)
            high.append(hi)
        low = jnp.transpose(jnp.concatenate(low, axis=0))
        high = jnp.transpose(jnp.concatenate(high, axis=0))
        table[:, SLOTS:] = jnp.concatenate([low, high[:COEFFS - SLOTS]], axis=0).astype(jnp.bfloat16)
        table[:, :SLOTS] = mult[...]
        listed = far_list[...]
        remote = listed - SLOTS
        compact = SLOTS + 32 * peer_slot(remote >> 5, device) + (remote & 31)
        compact = jnp.where(listed < SLOTS, listed, compact)
        entries[...] = jnp.transpose(compact.astype(jnp.float32)).astype(jnp.int32)
        local_out[...] = jnp.zeros_like(local_out)
        for axis in range(3):
            pos_t[axis] = jnp.transpose(pos[axis])
            coarse_t[axis] = jnp.transpose(coarse_coords[axis])
        before = iota((1, SLOTS), 1) < device
        start = jnp.sum(jnp.where(before, box_count[...].astype(jnp.float32), 0.0), axis=1, keepdims=True)
        start = jnp.broadcast_to(start.astype(jnp.int32), (TABLE, SLOTS))
        pieces = gy_recv[:, UNIT:UNIT + LEVEL3, :].reshape(TABLE, SLOTS)
        pieces = jnp.transpose(pieces.astype(jnp.float32)).astype(jnp.bfloat16)
        row = iota((TABLE, SLOTS), 0)
        member = (row >> 4) * 4 + (row & 3)
        hit = member == ((start + iota((TABLE, SLOTS), 1)) & 127)
        for half in range(2):
            order = jnp.where(hit & (((row >> 2) & 1) == half), 1.0, 0.0).astype(jnp.bfloat16)
            part = contract(pieces, order, (1, 0))
            if half:
                level3[SLOTS:, :] = part[:COEFFS - SLOTS]
            else:
                level3[:SLOTS, :] = part

    lines = iota((TABLE, SLOTS), 0).astype(jnp.int16)
    one, zero = jnp.ones((), jnp.bfloat16), jnp.zeros((), jnp.bfloat16)
    for pair in range(PER_STEP // 2):
        first = step * PER_STEP + 2 * pair
        hot = []
        for which in range(2):
            wanted = jnp.broadcast_to(entries[pl.ds(first + which, 1), :], (16, SLOTS)).astype(jnp.int16)
            wanted = jnp.concatenate([wanted] * (TABLE // 16), axis=0)
            hot.append(jnp.where(lines == wanted, one, zero))
        found = contract(table[...], jnp.concatenate(hot, axis=1), (1, 0))
        found = jnp.concatenate([found[:, :SLOTS], found[:, SLOTS:]], axis=0)
        picked[2 * COEFFS * pair:2 * COEFFS * (pair + 1), :] = found.astype(jnp.bfloat16)
    local_out[...] += contract(operators[...], picked[...], (1, 0))
    rows = 16
    for part in range(PER_STEP // rows):
        here = pl.ds(pl.multiple_of(step * PER_STEP + part * rows, rows), rows)
        both_t[here, :] = evaluate(level3, [coarse_t[axis, here, :] for axis in range(3)], rows)

    @pl.when(step == pl.num_programs(0) - 1)
    def _():
        @pl.loop(0, SLOTS // rows)
        def _(index):
            here = pl.ds(pl.multiple_of(index * rows, rows), rows)
            far = evaluate(local_out, [pos_t[axis, here, :] for axis in range(3)], rows)
            both_t[here, :] = both_t[here, :] + far

        eval_out[...] = jnp.transpose(both_t[...])


def far_field(mult, gy_recv, gx_recv, far_list, box_count, pos, coarse_coords, operators):
    steps = SLOTS // PER_STEP
    whole = pl.BlockSpec(memory_space=pltpu.VMEM)

    def const(shape):
        return pl.BlockSpec(shape, lambda i: (0,) * len(shape))

    return pl.pallas_call(
        far_kernel,
        grid=(steps,),
        out_shape=(
            jax.ShapeDtypeStruct((COEFFS, SLOTS), jnp.float32),
            jax.ShapeDtypeStruct((SLOTS, SLOTS), jnp.float32),
        ),
        in_specs=[whole] * 7 + [pl.BlockSpec((COEFFS, PER_STEP * COEFFS), lambda i: (0, i))],
        out_specs=(const((COEFFS, SLOTS)), const((SLOTS, SLOTS))),
        scratch_shapes=[
            pltpu.VMEM((COEFFS, TABLE), jnp.bfloat16),
            pltpu.VMEM((SLOTS, SLOTS), jnp.int32),
            pltpu.VMEM((PER_STEP * COEFFS, SLOTS), jnp.bfloat16),
            pltpu.VMEM((3, SLOTS, SLOTS), jnp.float32),
            pltpu.VMEM((3, SLOTS, SLOTS), jnp.float32),
            pltpu.VMEM((COEFFS, SLOTS), jnp.float32),
            pltpu.VMEM((SLOTS, SLOTS), jnp.float32),
        ],
        compiler_params=pltpu.CompilerParams(
            vmem_limit_bytes=56 * 1024 * 1024, dimension_semantics=("arbitrary",)
        ),
        name="far",
    )(mult, gy_recv, gx_recv, far_list, box_count, pos, coarse_coords, operators)


def split(value):
    high = value.astype(jnp.bfloat16).astype(jnp.float32)
    rest = value - high
    middle = rest.astype(jnp.bfloat16).astype(jnp.float32)
    return high, middle, rest - middle


class Near:
    scratch = [
        pltpu.VMEM((NEAR_ROWS, 64, SLOTS), jnp.bfloat16),
        pltpu.VMEM((27, 64, SLOTS), jnp.bfloat16),
        pltpu.VMEM((NEAR_ROWS, 8, SLOTS), jnp.float32),
        pltpu.VMEM((SLOTS, SLOTS, 48), jnp.bfloat16),
    ] + [
        pltpu.VMEM((48, max(FIRST, SECOND) * SLOTS), jnp.bfloat16),
        pltpu.VMEM((max(FIRST, SECOND), 8, SLOTS), jnp.float32),
    ] * TOGETHER

    def __init__(self, lists, pos, masked, out, source, moves, charge, target, *buffers):
        self.lists, self.pos, self.masked, self.out = lists, pos, masked, out
        self.source, self.moves, self.charge, self.target, self.buffers = source, moves, charge, target, buffers
        self.row8 = iota((8, SLOTS), 0)
        self.lag = iota((CHUNK, SLOTS), 1) - iota((CHUNK, SLOTS), 0)

    def stack(self, x, y, z, norm):
        value = jnp.where((self.row8 == 0) | (self.row8 == 5), x, norm)
        value = jnp.where((self.row8 == 1) | (self.row8 == 6), y, value)
        return jnp.where((self.row8 == 2) | (self.row8 == 7), z, value)

    def put_source(self, row, x, y, z, q):
        row8 = self.row8
        high, middle, low = split(self.stack(x, y, z, x * x + y * y + z * z))
        g1 = jnp.where(row8 >= 4, 1.0, high)
        g2 = jnp.where(row8 <= 3, middle, jnp.where(row8 == 4, 1.0, high))
        g3 = jnp.where(row8 <= 3, low, jnp.where(row8 == 4, 0.0, middle))
        g5 = jnp.where(row8 <= 4, middle, low)
        self.source[row, 0:48, :] = jnp.concatenate([g1, g2, g3, g1, g5, g1], axis=0).astype(jnp.bfloat16)
        self.charge[row] = q

    def put_target(self, box, x, y, z):
        row8 = self.row8
        norm = x * x + y * y + z * z + SOFTENING
        high, middle, low = split(self.stack(-2.0 * x, -2.0 * y, -2.0 * z, norm))
        c1 = jnp.where(row8 == 3, 1.0, high)
        c2 = jnp.where(row8 <= 2, high, 1.0)
        c4 = jnp.where(row8 == 3, 0.0, middle)
        c5 = jnp.where(row8 <= 2, middle, jnp.where(row8 <= 4, 0.0, 1.0))
        c6 = jnp.where(row8 == 3, 0.0, low)
        columns = jnp.concatenate([c1, c2, c2, c4, c5, c6], axis=0)
        self.target[box] = jnp.transpose(columns).astype(jnp.bfloat16)

    def tables(self):
        @pl.loop(0, SLOTS // 16)
        def _(group):
            for which in range(16):
                box = 16 * group + which
                here = pl.ds(box, 1)
                x, y, z = [jnp.broadcast_to(self.pos[axis, here, :], (8, SLOTS)) for axis in range(3)]
                self.put_source(box, x, y, z, jnp.broadcast_to(self.masked[here, :], (8, SLOTS)))
                self.put_target(box, x, y, z)

        none = jnp.zeros((8, SLOTS), jnp.float32)
        self.put_source(EMPTY, none, none, none, none)
        row8 = self.row8
        for code in range(27):
            move = [2.0 * (code // 9 - 1), 2.0 * (code // 3 % 3 - 1), 2.0 * (code % 3 - 1)]
            shift = jnp.full((8, SLOTS), 1.0, jnp.float32)
            for axis in range(3):
                shift = jnp.where(row8 == 5 + axis, move[axis], shift)
            twice = jnp.where(row8 >= 5, 2.0 * shift, shift)
            square = jnp.where(row8 == 4, sum(m * m for m in move), twice)
            groups = jnp.concatenate([shift, square, twice, shift, twice, shift], axis=0)
            self.moves[code, 0:48, :] = groups.astype(jnp.bfloat16)

    def remote(self, messages):
        for j, (message, valid) in enumerate(messages):
            value = message[64:UNIT, :].astype(jnp.float32)
            for block in range(8):
                rows = [value[8 * field + block:8 * field + block + 1] for field in range(4)]
                self.put_source(SLOTS + 8 * j + block, *[jnp.broadcast_to(row, (8, SLOTS)) for row in rows])

    def prepare(self, box, rows_at, moves_at, width, rhs, q):
        for n in range(width):
            row, move = self.lists[box, rows_at + n], self.lists[box, moves_at + n]
            rhs[:, SLOTS * n:SLOTS * n + SLOTS] = self.source[row, 0:48, :] * self.moves[move, 0:48, :]
            q[n] = self.charge[row]

    def compute(self, box, width, rhs, q, rows, first):
        for base in range(0, rows, CHUNK):
            size = min(CHUNK, rows - base)
            mine = self.target[box, base:base + size, :]
            acc = jnp.zeros((size, SLOTS), jnp.float32)
            for pair in range(width // 2):
                dist = contract(mine, rhs[:, 256 * pair:256 * pair + 256], (1, 0))
                kernel = lax.rsqrt(dist)
                for which in range(2):
                    n = 2 * pair + which
                    part = kernel[:, SLOTS * which:SLOTS * which + SLOTS]
                    if first and n == 0:
                        part = jnp.where(self.lag[:size] == base, 0.0, part)
                    acc = acc + part * jnp.concatenate([q[n]] * (size // 8), axis=0)
            value = jnp.sum(jnp.transpose(acc), axis=0, keepdims=True)
            here = pl.ds(box, 1), slice(base, base + size)
            self.out[here] = value if first else self.out[here] + value

    def run(self, rows_at, moves_at, width, order, first, together):
        begin = 0
        for chunks in (4, 3, 2, 1):
            end = (self.lists[chunks, order + 1] + together - 1) // together

            @pl.loop(begin, end)
            def _(group):
                boxes = [self.lists[together * group + which, order] for which in range(together)]
                for which in range(together):
                    self.prepare(boxes[which], rows_at, moves_at, width, *self.buffers[2 * which:2 * which + 2])
                for which in range(together):
                    self.compute(boxes[which], width, *self.buffers[2 * which:2 * which + 2], 32 * chunks, first)

            begin = jnp.maximum(begin, end)


def near_own_kernel(lists, pos, masked, after, out, *scratch):
    near = Near(lists, pos, masked, out, *scratch)
    near.tables()
    near.run(0, FIRST, FIRST, ORDER_AT, True, TOGETHER)


def near_kernel(lists, pos, masked, gy_recv, gx_recv, near_in, eval_in, count_row, out, *scratch):
    near = Near(lists, pos, masked, out, *scratch)
    near.tables()
    near.remote(peers(gy_recv, gx_recv, *position()))
    out[...] = near_in[...] + eval_in[...]

    for part in range(2):
        rows_at = 2 * FIRST + SECOND * part
        near.run(rows_at, rows_at + 2 * SECOND, SECOND, ORDER_AT + 2 * part, False, TOGETHER // (1 + part))

    count_col = jnp.transpose(jnp.broadcast_to(count_row[...], (SLOTS, SLOTS)).astype(jnp.float32))
    live = iota((SLOTS, SLOTS), 1).astype(jnp.float32) < count_col
    out[...] = jnp.where(live, out[...], 0.0)


def near_own(lists, pos, masked, after):
    whole = pl.BlockSpec(memory_space=pltpu.VMEM)
    return pl.pallas_call(
        near_own_kernel,
        out_shape=jax.ShapeDtypeStruct((SLOTS, SLOTS), jnp.float32),
        in_specs=[pl.BlockSpec(memory_space=pltpu.SMEM), whole, whole, pl.BlockSpec(memory_space=pl.ANY)],
        out_specs=whole,
        scratch_shapes=Near.scratch,
        compiler_params=VMEM,
        cost_estimate=pl.CostEstimate(flops=10**9, bytes_accessed=6 * 10**7, transcendentals=2 * 10**7),
        name="near_own",
    )(lists, pos, masked, after)


def near_field(lists, pos, masked, gy_recv, gx_recv, near_in, eval_in, count_row):
    whole = pl.BlockSpec(memory_space=pltpu.VMEM)
    return pl.pallas_call(
        near_kernel,
        out_shape=jax.ShapeDtypeStruct((SLOTS, SLOTS), jnp.float32),
        in_specs=[pl.BlockSpec(memory_space=pltpu.SMEM)] + [whole] * 7,
        out_specs=whole,
        scratch_shapes=Near.scratch,
        compiler_params=VMEM,
        name="near",
    )(lists, pos, masked, gy_recv, gx_recv, near_in, eval_in, count_row)


def on_device(
    multipoles,
    operators,
    coarse_local,
    positions,
    charges,
    coarse_coords,
    box_count,
    particle_count,
    expansion_sends,
    far_list,
    block_sends,
    near_list,
    near_offset,
):
    mult = multipoles.T
    pos = jnp.transpose(positions, (1, 0, 2))
    coarse_pos = jnp.transpose(coarse_coords, (1, 0, 2))
    count_row = particle_count.reshape(1, SLOTS)
    box_row = box_count.reshape(1, SLOTS)
    gy_buffer, gx_buffer, masked, lists = pack(
        mult, expansion_sends[0].T, block_sends[0].T, pos, charges, count_row, coarse_local,
        near_list.T, near_offset.T,
    )
    gx_recv = lax.all_to_all(gx_buffer, "gx", 0, 0, tiled=True)
    gy_buffer = forward(gy_buffer, gx_recv, box_row)
    near = near_own(lists, pos, masked, gy_buffer)
    gy_recv = lax.all_to_all(gy_buffer, "gy", 0, 0, tiled=True)
    local_exp, evaluated = far_field(mult, gy_recv, gx_recv, far_list, box_row, pos, coarse_pos, operators)
    potential = near_field(lists, pos, masked, gy_recv, gx_recv, near, evaluated, count_row)
    return (potential, local_exp)


def solution(mesh):
    both = ("gx", "gy")
    in_specs = (
        P(both, None),
        P(),
        P(both, None),
        P(both, None, None),
        P(both, None),
        P(both, None, None),
        P(),
        P(both),
        P(both, None, None),
        P(both, None),
        P(both, None, None),
        P(both, None),
        P(both, None),
    )
    out_specs = (P(both, None), P(None, both))
    return jax.shard_map(
        on_device, mesh=mesh, in_specs=in_specs, out_specs=out_specs, check_vma=False
    )
```
